256 devices in a mesh: dp: 16 (over z_hi, x), grp: 4 (over z_lo, core), rep: 4 (over y).
Axes of the slice: x: 4, y: 4, z: 8 (z_hi: 4, z_lo: 2; z = z_hi * 2 + z_lo), core: 2. Of those that a mesh axis runs over, the one named last changes fastest.
Arguments:
- activations: bfloat16 [32768, 4096], P(('dp', 'grp', 'rep')), may hold values from -60 to 60
- out_grads: bfloat16 [32768, 10240], P(('dp', 'grp', 'rep')), may hold values from -60 to 60
- a_running: float32 [16, 256, 256], replicated, may hold values from -40 to 60, as said below
- g_running: float32 [32, 320, 320], P('dp'), may hold values from -40 to 60, as said below
- grad_partial: bfloat16 [4, 4096, 10240], P('rep', 'grp', 'dp'), may hold values from -96 to 96
Outputs:
- preconditioned: bfloat16 [4096, 10240], P('grp', 'dp')
The draws below stay inside these ranges and needn't reach their ends.
Inputs may be any that keep to these rules, and one draw needn't show every extreme that they name: `a_running`: each block is symmetric positive definite. `g_running`: each block is symmetric positive definite.
All inputs are finite; a program needn't handle non-finite values.
Results may differ from the reference program's by a relative error of at most 0.001.
Values may be sent and summed in bfloat16 or wider, within the bound.
No kernel may reach another device: no remote copies, remote signals or barrier semaphores. Data moves between devices by JAX's collectives and lax.ppermute only.
A program may use at most 128 MiB of HBM per device.

```python
import math
import jax
import jax.numpy as jnp
from jax import lax

D = 4096
FF = 10240
BA = 256
BG = 320
ITERS = 8
NA = 16
NG = 32
TOKENS = 32768
REPLICAS = 4


def scaled_rows(base_draw, key_rows, key_cols, top_row, top_col):
    rows_scale = jnp.exp(jax.random.uniform(key_rows, (base_draw.shape[0], 1), minval=0.0, maxval=math.log(top_row)))
    cols_scale = jnp.exp(jax.random.uniform(key_cols, (1, base_draw.shape[1]), minval=0.0, maxval=math.log(top_col)))
    return base_draw * rows_scale * cols_scale


def spd_blocks(key, block_count, block_size, top_scale):
    key_off, key_diag, key_scale = jax.random.split(key, 3)
    uniform_off = jax.random.uniform(key_off, (block_count, block_size, block_size), minval=-1.0, maxval=1.0)
    symmetric = 0.5 * (uniform_off + jnp.swapaxes(uniform_off, 1, 2))
    identity = jnp.eye(block_size, dtype=jnp.float32)
    diag_part = 1.05 + 0.3 * jax.random.uniform(key_diag, (block_count, block_size, 1))
    inner_part = identity[None] * diag_part + (1.0 - identity[None]) * symmetric / block_size
    scales = jnp.exp(jax.random.uniform(key_scale, (block_count, block_size), minval=0.0, maxval=math.log(top_scale)))
    return scales[:, :, None] * scales[:, None, :] * inner_part


def draw_activations(key, part):
    key = jax.random.fold_in(key, 11)
    key_base, key_rows, key_cols = jax.random.split(key, 3)
    base_draw = jnp.clip(jax.random.normal(key_base, (TOKENS, D)), -5.0, 5.0)
    return scaled_rows(base_draw, key_rows, key_cols, 3.0, 3.2).astype(jnp.bfloat16)


def draw_out_grads(key, part):
    key = jax.random.fold_in(key, 23)
    key_base, key_rows, key_cols = jax.random.split(key, 3)
    base_draw = jnp.clip(jax.random.normal(key_base, (TOKENS, FF)), -5.0, 5.0)
    return scaled_rows(base_draw, key_rows, key_cols, 3.0, 3.2).astype(jnp.bfloat16)


def draw_a_running(key, part):
    key = jax.random.fold_in(key, 37)
    return spd_blocks(key, NA, BA, 3.2)


def draw_g_running(key, part):
    key = jax.random.fold_in(key, 41)
    return spd_blocks(key, NG, BG, 3.2)


def levels(own_key, shape, pieces, least, largest):
    level, own = 1.0, jax.random.fold_in(own_key, 6)
    for dim, parts in pieces:
        heights = jnp.exp(jax.random.uniform(jax.random.fold_in(own, dim), (parts,), jnp.float32, least / len(pieces), largest / len(pieces)))
        level = level * jnp.repeat(heights, shape[dim] // parts).reshape([-1 if axis == dim else 1 for axis in range(len(shape))])
    return level


def centred(rng, extent, scale, limit, cuts=(), held_as=jnp.bfloat16):
    entries = scale * jax.random.normal(rng, extent, jnp.float32)
    if cuts:
        entries = entries * levels(rng, extent, cuts, -0.22, 0.18)
    return jnp.clip(entries, -limit, limit).astype(held_as)


def setup_inputs(seed: int = 0) -> dict:
    keys = jax.random.split(jax.random.key(seed), 6)
    return {
        "activations": draw_activations(jax.random.fold_in(keys[5], 71), 0),
        "out_grads": draw_out_grads(jax.random.fold_in(keys[5], 71), 0),
        "a_running": draw_a_running(jax.random.fold_in(keys[5], 71), 0),
        "g_running": draw_g_running(jax.random.fold_in(keys[5], 71), 0),
        "grad_partial": centred(keys[4], (REPLICAS, D, FF), 16.0, 96.0, ((0, 4), (1, 4), (2, 16))),
    }


factor_decay = 0.9
damping = 0.1


def block_cov(samples, block_size):
    block_count = samples.shape[1] // block_size

    def one_block(block_index):
        column_block = lax.dynamic_slice_in_dim(samples, block_index * block_size, block_size, 1)
        return lax.dot_general(column_block, column_block, (((0,), (0,)), ((), ())), preferred_element_type=jnp.float32)

    return lax.map(one_block, jnp.arange(block_count, dtype=jnp.int32))


def damped_factor(previous, new_sum, token_total):
    identity = jnp.eye(previous.shape[-1], dtype=jnp.float32)
    mixed = factor_decay * previous + (1.0 - factor_decay) * new_sum / token_total
    return mixed + damping * identity


def inverse_newton(matrices):
    identity = jnp.eye(matrices.shape[-1], dtype=jnp.float32)
    trace_sum = jnp.sum(matrices * identity, axis=(1, 2))
    approx = identity[None, :, :] / trace_sum[:, None, None]
    for _ in range(ITERS):
        product = jnp.einsum("nij,njk->nik", matrices, approx, precision=lax.Precision.HIGHEST)
        approx = jnp.einsum("nij,njk->nik", approx, 2.0 * identity - product, precision=lax.Precision.HIGHEST)
    return approx


def reference(activations, out_grads, a_running, g_running, grad_partial):
    token_total = activations.shape[0]
    a_inverse = inverse_newton(damped_factor(a_running, block_cov(activations, BA), token_total))
    g_inverse = inverse_newton(damped_factor(g_running, block_cov(out_grads, BG), token_total))
    summed = jnp.sum(grad_partial.astype(jnp.float32), axis=0)
    blocks = summed.reshape(NA, BA, NG, BG)
    left_done = jnp.einsum("aij,ajgk->aigk", a_inverse, blocks, precision=lax.Precision.HIGHEST)
    both_done = jnp.einsum("aigk,gkl->aigl", left_done, g_inverse, precision=lax.Precision.HIGHEST)
    return both_done.reshape(D, FF).astype(jnp.bfloat16)
```

```python
import jax
import jax.numpy as jnp
from jax import lax
from jax.sharding import Mesh, PartitionSpec as P

BA = 256
BG = 320
ITERS = 8

factor_decay = 0.9
damping = 0.1


def swap_cores(value):
    return lax.ppermute(value, "c", [(0, 1), (1, 0)])


def send_round(axis, chunk_for):
    size = lax.axis_size(axis)
    here = lax.axis_index(axis)
    out = [chunk_for(here)]
    for shift in range(1, size):
        chunk = chunk_for(lax.rem(here + shift, size))
        out.append(lax.ppermute(chunk, axis, [(i, (i + shift) % size) for i in range(size)]))
    return out


def damped_factor(previous, new_sum, token_total):
    identity = jnp.eye(previous.shape[-1], dtype=jnp.float32)
    mixed = factor_decay * previous + (1.0 - factor_decay) * new_sum / token_total
    return mixed + damping * identity


def inverse_newton(matrices):
    identity = jnp.eye(matrices.shape[-1], dtype=jnp.float32)
    trace_sum = jnp.sum(matrices * identity, axis=(1, 2))
    approx = identity[None, :, :] / trace_sum[:, None, None]
    for _ in range(ITERS):
        product = jnp.einsum("nij,njk->nik", matrices, approx, precision=lax.Precision.HIGHEST)
        approx = jnp.einsum(
            "nij,njk->nik", approx, 2.0 * identity - product, precision=lax.Precision.HIGHEST
        )
    return approx


def reduce_pieces(value, axes):
    return jnp.sum(lax.all_to_all(value, axes, 0, 0, tiled=True), axis=0)


def gather_pieces(value, axes):
    size = lax.axis_size(axes)
    every = jnp.broadcast_to(value[None], (size, *value.shape))
    return lax.all_to_all(every, axes, 0, 0, tiled=True)


def per_device(activations, out_grads, a_running, g_running, grad_partial):
    token_total = float(activations.shape[0] * 256)
    zl, c, y = lax.axis_index("zl"), lax.axis_index("c"), lax.axis_index("y")

    def g_chunk(xi):
        return jnp.stack([
            lax.dynamic_slice_in_dim(out_grads, (zh * 4 + xi) * 2 * BG, 2 * BG, 1) for zh in range(4)
        ])

    def a_chunk(yi):
        return jnp.stack([
            lax.dynamic_slice_in_dim(activations, (q * 4 + yi) * BA, BA, 1) for q in range(4)
        ])

    def grad_chunk(yi):
        return lax.dynamic_slice_in_dim(grad_partial[0], yi * BA, BA, 0)

    g_all = jnp.concatenate(send_round("x", g_chunk), axis=1)
    a_all = jnp.concatenate(send_round("y", a_chunk), axis=1)
    grads = send_round("y", grad_chunk)

    ga = g_all[:, :, :BG]
    gb = g_all[:, :, BG:]
    g_mine = jnp.where(c == 0, ga, gb)
    g_other = jnp.where(c == 0, gb, ga)
    cov = lambda v: jnp.einsum("ntb,ntc->nbc", v, v, preferred_element_type=jnp.float32)
    g_cov = cov(g_mine) + swap_cores(cov(g_other))
    a_cov_all = cov(a_all).reshape(2, 2, BA, BA)
    a_mine = lax.dynamic_index_in_dim(a_cov_all, c, 1, keepdims=False)
    a_other = lax.dynamic_index_in_dim(a_cov_all, 1 - c, 1, keepdims=False)
    a_cov = a_mine + swap_cores(a_other)

    a_piece = reduce_pieces(a_cov.reshape(32, 16, BA), ("zl", "zh", "x"))
    a_owned = gather_pieces(a_piece, ("zh", "x")).reshape(1, BA, BA)
    g_piece = reduce_pieces(g_cov.reshape(32, 40, BG), ("zh", "zl", "y"))
    g_owned = gather_pieces(g_piece, ("c", "zl", "y")).reshape(2, BG, BG)

    block = (zl * 2 + c) * 4 + y
    a_previous = lax.dynamic_slice_in_dim(a_running, block, 1, 0)
    a_inverse = inverse_newton(damped_factor(a_previous, a_owned, token_total))[0]
    g_inverse = inverse_newton(damped_factor(g_running, g_owned, token_total))

    summed = sum(v.astype(jnp.float32) for v in grads)
    left = jnp.dot(a_inverse, summed, precision=lax.Precision.HIGHEST)
    both = jnp.concatenate([
        jnp.dot(left[:, k * BG:(k + 1) * BG], g_inverse[k], precision=lax.Precision.HIGHEST)
        for k in range(2)
    ], axis=1)
    rows = both.astype(jnp.bfloat16)

    out = jnp.zeros((4, BA, 2 * BG), jnp.bfloat16)
    for shift, got in enumerate(send_round("y", lambda i: rows)):
        out = lax.dynamic_update_slice_in_dim(out, got[None], lax.rem(y + 4 - shift, 4), 0)
    return out.reshape(4 * BA, 2 * BG)


def solution(mesh):
    fine = Mesh(mesh.devices.reshape(4, 4, 2, 2, 4), ("zh", "x", "zl", "c", "y"))
    tokens = P(("zh", "x", "zl", "c", "y"), None)
    placed = (tokens, tokens, P(), P(("zh", "x"), None, None), P("y", ("zl", "c"), ("zh", "x")))
    return jax.shard_map(
        per_device,
        mesh=fine,
        in_specs=placed,
        out_specs=P(("zl", "c"), ("zh", "x")),
        check_vma=False,
    )
```

```python
import functools

import jax
import jax.numpy as jnp
from jax import lax
from jax.experimental import pallas as pl
from jax.experimental.pallas import tpu as pltpu
from jax.sharding import Mesh, PartitionSpec as P

BA = 256
BG = 320
BGP = 384
ITERS = 8
G_TILES = 112
A_TILES = 48

factor_decay = 0.9
damping = 0.1

ANY = pl.BlockSpec(memory_space=pl.ANY)
VMEM = pl.BlockSpec(memory_space=pltpu.VMEM)


def swap_cores(value):
    return lax.ppermute(value, "c", [(0, 1), (1, 0)])


def send_round(axis, chunks):
    size = lax.axis_size(axis)
    return [chunks[0]] + [
        lax.ppermute(chunks[s], axis, [(i, (i + s) % size) for i in range(size)])
        for s in range(1, size)
    ]


def pack_kernel(axis, width, src, *rest):
    outs, sem = rest[:4], rest[4]
    here = lax.axis_index(axis)
    copies = []
    for s in (1, 2, 3, 0):
        peer = lax.rem(here + s, 4)
        for q in range(4):
            start = pl.multiple_of((q * 4 + peer) * width, 128)
            copies.append(pltpu.make_async_copy(
                src.at[:, pl.ds(start, width)], outs[s].at[q], sem.at[s * 4 + q]
            ))
    for copy in copies:
        copy.start()
    for copy in copies:
        copy.wait()


def pack(samples, axis, width):
    piece = jax.ShapeDtypeStruct((4, samples.shape[0], width), samples.dtype)
    return pl.pallas_call(
        functools.partial(pack_kernel, axis, width),
        out_shape=[piece] * 4,
        in_specs=[ANY],
        out_specs=[ANY] * 4,
        scratch_shapes=[pltpu.SemaphoreType.DMA((16,))],
    )(samples)


def gram(v):
    return lax.dot_general(v, v, (((0,), (0,)), ((), ())), preferred_element_type=jnp.float32)


def grid_of(n):
    return (lax.broadcasted_iota(jnp.int32, (n, n), 0), lax.broadcasted_iota(jnp.int32, (n, n), 1))


def g_cov_kernel(i0, i1, i2, i3, own, other, rows, tiles):
    c = lax.axis_index("c")
    for s, ref in enumerate((i0, i1, i2, i3)):
        rows[s * 128:(s + 1) * 128, :] = ref[0]
    first = gram(rows[:, 0:BGP])[:BG, :BG]
    second = gram(rows[:, 2 * BG - BGP:2 * BG])[BGP - BG:, BGP - BG:]
    r, k = grid_of(BG)
    fold = jnp.where(r >= k, first, second)
    diag = jnp.sum(jnp.where(r == k, second, 0.0), axis=0, keepdims=True)
    half = BG // 2
    wide = jnp.concatenate([fold[:half], fold[half:]], axis=1)
    tail = jnp.concatenate([jnp.broadcast_to(diag, (8, BG)), jnp.zeros((8, BG), jnp.float32)], axis=1)
    for l in range(5):
        tiles[l * 21:l * 21 + 20] = wide[:, l * 128:(l + 1) * 128].reshape(20, 8, 128)
        tiles[l * 21 + 20] = tail[:, l * 128:(l + 1) * 128]
    tiles[105:] = jnp.zeros((7, 8, 128), jnp.float32)
    own[0] = tiles[pl.ds(c * 56, 56)]
    other[0] = tiles[pl.ds((1 - c) * 56, 56)]


def g_cov(chunks):
    spec = pl.BlockSpec((1, 128, 2 * BG), lambda q: (q, 0, 0))
    out = pl.BlockSpec((1, 56, 8, 128), lambda q: (q, 0, 0, 0))
    return pl.pallas_call(
        g_cov_kernel,
        grid=(4,),
        out_shape=[jax.ShapeDtypeStruct((4, 56, 8, 128), jnp.float32)] * 2,
        in_specs=[spec] * 4,
        out_specs=[out] * 2,
        scratch_shapes=[pltpu.VMEM((512, 2 * BG), jnp.bfloat16), pltpu.VMEM((G_TILES, 8, 128), jnp.float32)],
        compiler_params=pltpu.CompilerParams(vmem_limit_bytes=32 << 20),
    )(*chunks)


def a_cov_kernel(i0, i1, i2, i3, own, other, rows):
    c = lax.axis_index("c")
    r, k = grid_of(128)
    for zl in range(2):
        for which, out in ((c, own), (1 - c, other)):
            q = zl * 2 + which
            for s, ref in enumerate((i0, i1, i2, i3)):
                rows[s * 128:(s + 1) * 128, :] = ref[q]
            cov = gram(rows[...])
            corner = cov[128:, 128:]
            fold = jnp.where(r >= k, cov[:128, :128], corner)
            diag = jnp.sum(jnp.where(r == k, corner, 0.0), axis=0, keepdims=True)
            out[zl, 0:16] = cov[128:, :128].reshape(16, 8, 128)
            out[zl, 16:32] = fold.reshape(16, 8, 128)
            out[zl, 32] = jnp.broadcast_to(diag, (8, 128))
            out[zl, 33:] = jnp.zeros((A_TILES - 33, 8, 128), jnp.float32)


def a_cov(chunks):
    return pl.pallas_call(
        a_cov_kernel,
        out_shape=[jax.ShapeDtypeStruct((2, A_TILES, 8, 128), jnp.float32)] * 2,
        in_specs=[VMEM] * 4,
        out_specs=[VMEM] * 2,
        scratch_shapes=[pltpu.VMEM((512, BA), jnp.bfloat16)],
        compiler_params=pltpu.CompilerParams(vmem_limit_bytes=32 << 20),
    )(*chunks)


def reduce_pieces(value, axes):
    return jnp.sum(lax.all_to_all(value, axes, 0, 0, tiled=True), axis=0)


def gather_pieces(value, axes):
    size = lax.axis_size(axes)
    every = jnp.broadcast_to(value[None], (size, *value.shape))
    return lax.all_to_all(every, axes, 0, 0, tiled=True)


def split(value):
    high = value.astype(jnp.bfloat16)
    return high, (value - high.astype(jnp.float32)).astype(jnp.bfloat16)


def dot3(left, right):
    dot = functools.partial(jnp.dot, preferred_element_type=jnp.float32)
    return dot(left[0], right[0]) + (dot(left[0], right[1]) + dot(left[1], right[0]))


def newton(matrices, identity):
    n = identity.shape[0]
    state = []
    for matrix in matrices:
        trace = jnp.sum(matrix * identity)
        scaled = matrix / trace
        step = 2.0 * identity - scaled
        state.append((step / trace, dot3(split(scaled), split(step))))
    for _ in range(ITERS - 2):
        following = []
        for approx, product in state:
            both = dot3(split(jnp.concatenate([approx, product], axis=0)), split(2.0 * identity - product))
            following.append((both[:n], both[n:]))
        state = following
    return [dot3(split(approx), split(2.0 * identity - product)) for approx, product in state]


def a_side_kernel(tiles, running, g0, g1, g2, g3, left, *, token_total):
    r, k = grid_of(128)
    low = tiles[0:16].reshape(128, 128)
    fold = tiles[16:32].reshape(128, 128)
    diag = tiles[32][0:1]
    turned = fold.T
    top = jnp.where(r >= k, fold, turned)
    corner = jnp.where(r == k, jnp.broadcast_to(diag, (128, 128)), jnp.where(r < k, fold, turned))
    cov = jnp.concatenate([
        jnp.concatenate([top, low.T], axis=1), jnp.concatenate([low, corner], axis=1)
    ], axis=0)
    r, k = grid_of(BA)
    identity = jnp.where(r == k, 1.0, 0.0)
    mixed = factor_decay * running[0] + (1.0 - factor_decay) * cov / token_total
    inverse, = newton([mixed + damping * identity], identity)
    summed = (g0[...].astype(jnp.float32) + g1[...].astype(jnp.float32)) + (
        g2[...].astype(jnp.float32) + g3[...].astype(jnp.float32)
    )
    left[...] = dot3(split(inverse), split(summed))


def a_side(tiles, running, grads, token_total):
    return pl.pallas_call(
        functools.partial(a_side_kernel, token_total=token_total),
        out_shape=jax.ShapeDtypeStruct((BA, 2 * BG), jnp.float32),
        in_specs=[VMEM] * 6,
        out_specs=VMEM,
        compiler_params=pltpu.CompilerParams(vmem_limit_bytes=32 << 20),
        cost_estimate=pl.CostEstimate(flops=2_500_000_000, bytes_accessed=2_000_000, transcendentals=0),
    )(tiles, running, *grads)


def g_side_kernel(tiles, running, left, out, fold, wide, *, token_total):
    half = BG // 2
    for l in range(5):
        wide[:, l * 128:(l + 1) * 128] = tiles[l * 21:(l + 1) * 21].reshape(168, 128)
    fold[...] = jnp.zeros((BGP, BGP), jnp.float32)
    fold[0:half, 0:BG] = wide[0:half, 0:BG]
    fold[half:BG, 0:BG] = wide[0:half, BG:]
    diag = jnp.concatenate([wide[half:half + 1, 0:BG], jnp.zeros((1, BGP - BG), jnp.float32)], axis=1)
    r, k = grid_of(BGP)
    held = fold[...]
    turned = held.T
    first = jnp.where(r >= k, held, turned)
    second = jnp.where(r == k, jnp.broadcast_to(diag, (BGP, BGP)), jnp.where(r < k, held, turned))
    identity = jnp.where((r == k) & (r < BG), 1.0, 0.0)
    matrices = []
    for n, cov in enumerate((first, second)):
        fold[0:BG, 0:BG] = running[n]
        mixed = factor_decay * fold[...] + (1.0 - factor_decay) * cov / token_total
        matrices.append(mixed + damping * identity)
    inverse = newton(matrices, identity)
    for n in range(2):
        part = left[:, n * BG:(n + 1) * BG]
        done = dot3(split(part), split(inverse[n][:BG, :BG]))
        out[:, n * BG:(n + 1) * BG] = done.astype(jnp.bfloat16)


def g_side(tiles, running, left, token_total):
    return pl.pallas_call(
        functools.partial(g_side_kernel, token_total=token_total),
        out_shape=jax.ShapeDtypeStruct((BA, 2 * BG), jnp.bfloat16),
        in_specs=[VMEM] * 3,
        out_specs=VMEM,
        scratch_shapes=[pltpu.VMEM((BGP, BGP), jnp.float32), pltpu.VMEM((168, 2 * BG), jnp.float32)],
        compiler_params=pltpu.CompilerParams(vmem_limit_bytes=40 << 20),
        cost_estimate=pl.CostEstimate(flops=10_000_000_000, bytes_accessed=3_000_000, transcendentals=0),
    )(tiles, running, left)


def per_device(activations, out_grads, a_running, g_running, grad_partial):
    token_total = float(activations.shape[0] * 256)
    zl, c, y = lax.axis_index("zl"), lax.axis_index("c"), lax.axis_index("y")

    g_in = send_round("x", pack(out_grads, "x", 2 * BG))
    a_in = send_round("y", pack(activations, "y", BA))
    grads = send_round("y", [
        lax.dynamic_slice_in_dim(grad_partial[0], lax.rem(y + s, 4) * BA, BA, 0) for s in range(4)
    ])

    a_own, a_other = a_cov(a_in)
    a_part = a_own + swap_cores(a_other)
    a_piece = reduce_pieces(a_part.reshape(32, A_TILES // 2, 128), ("zl", "zh", "x"))
    a_tiles = gather_pieces(a_piece, ("zh", "x")).reshape(A_TILES, 8, 128)

    g_in, a_tiles, grads = lax.optimization_barrier((g_in, a_tiles, grads))
    g_own, g_other = g_cov(g_in)
    g_part = g_own + swap_cores(g_other)
    g_piece = reduce_pieces(g_part.reshape(32, 56, 128), ("zh", "zl", "y"))
    g_tiles = gather_pieces(g_piece, ("c", "zl", "y")).reshape(G_TILES, 8, 128)

    a_previous = lax.dynamic_slice_in_dim(a_running, (zl * 2 + c) * 4 + y, 1, 0)
    left = a_side(a_tiles, a_previous, grads, token_total)
    rows = g_side(g_tiles, g_running, left, token_total)

    out = jnp.zeros((4, BA, 2 * BG), jnp.bfloat16)
    for shift, got in enumerate(send_round("y", [rows] * 4)):
        out = lax.dynamic_update_slice_in_dim(out, got[None], lax.rem(y + 4 - shift, 4), 0)
    return out.reshape(4 * BA, 2 * BG)


def solution(mesh):
    fine = Mesh(mesh.devices.reshape(4, 4, 2, 2, 4), ("zh", "x", "zl", "c", "y"))
    tokens = P(("zh", "x", "zl", "c", "y"), None)
    placed = (tokens, tokens, P(), P(("zh", "x"), None, None), P("y", ("zl", "c"), ("zh", "x")))
    return jax.shard_map(
        per_device,
        mesh=fine,
        in_specs=placed,
        out_specs=P(("zl", "c"), ("zh", "x")),
        check_vma=False,
    )
```

```python
import functools

import jax
import jax.numpy as jnp
from jax import lax
from jax.experimental import pallas as pl
from jax.experimental.pallas import tpu as pltpu
from jax.sharding import Mesh, PartitionSpec as P

BA = 256
BG = 320
BGP = 384
ITERS = 8
G_TILES = 112
A_TILES = 48

factor_decay = 0.9
damping = 0.1

VMEM = pl.BlockSpec(memory_space=pltpu.VMEM)


def swap_cores(value):
    return lax.ppermute(value, "c", [(0, 1), (1, 0)])


def send_round(axis, chunks):
    size = lax.axis_size(axis)
    return [chunks[0]] + [
        lax.ppermute(chunks[s], axis, [(i, (i + s) % size) for i in range(size)])
        for s in range(1, size)
    ]


def pack_kernel(axis, width, src, *rest):
    outs, sem = rest[:4], rest[4]
    here = lax.axis_index(axis)
    copies = []
    for s in (1, 3, 2, 0):
        peer = lax.rem(here + s, 4)
        for q in range(4):
            start = pl.multiple_of((q * 4 + peer) * width, 128)
            copies.append(pltpu.make_async_copy(
                src.at[:, pl.ds(start, width)], outs[s].at[q], sem.at[s * 4 + q]
            ))
    for copy in copies:
        copy.start()
    for copy in copies:
        copy.wait()


def pack(samples, axis, width):
    piece = jax.ShapeDtypeStruct((4, samples.shape[0], width), samples.dtype)
    return pl.pallas_call(
        functools.partial(pack_kernel, axis, width),
        out_shape=[piece] * 4,
        in_specs=[pl.BlockSpec(memory_space=pl.ANY)],
        out_specs=[VMEM] * 4,
        scratch_shapes=[pltpu.SemaphoreType.DMA((16,))],
    )(samples)


def gram(v):
    return lax.dot_general(v, v, (((0,), (0,)), ((), ())), preferred_element_type=jnp.float32)


def grid_of(n):
    return (lax.broadcasted_iota(jnp.int32, (n, n), 0), lax.broadcasted_iota(jnp.int32, (n, n), 1))


def g_cov_kernel(i0, i1, i2, i3, own, other, rows, tiles):
    c = lax.axis_index("c")
    for s, ref in enumerate((i0, i1, i2, i3)):
        rows[s * 128:(s + 1) * 128, :] = ref[0]
    first = gram(rows[:, 0:BGP])[:BG, :BG]
    second = gram(rows[:, 2 * BG - BGP:2 * BG])[BGP - BG:, BGP - BG:]
    r, k = grid_of(BG)
    fold = jnp.where(r >= k, first, second)
    diag = jnp.sum(jnp.where(r == k, second, 0.0), axis=0, keepdims=True)
    half = BG // 2
    wide = jnp.concatenate([fold[:half], fold[half:]], axis=1)
    tail = jnp.concatenate([jnp.broadcast_to(diag, (8, BG)), jnp.zeros((8, BG), jnp.float32)], axis=1)
    for l in range(5):
        tiles[l * 21:l * 21 + 20] = wide[:, l * 128:(l + 1) * 128].reshape(20, 8, 128)
        tiles[l * 21 + 20] = tail[:, l * 128:(l + 1) * 128]
    tiles[105:] = jnp.zeros((7, 8, 128), jnp.float32)
    own[0] = tiles[pl.ds(c * 56, 56)]
    other[0] = tiles[pl.ds((1 - c) * 56, 56)]


def g_cov(chunks):
    spec = pl.BlockSpec((1, 128, 2 * BG), lambda q: (q, 0, 0))
    out = pl.BlockSpec((1, 56, 8, 128), lambda q: (q, 0, 0, 0))
    return pl.pallas_call(
        g_cov_kernel,
        grid=(4,),
        out_shape=[jax.ShapeDtypeStruct((4, 56, 8, 128), jnp.float32)] * 2,
        in_specs=[spec] * 4,
        out_specs=[out] * 2,
        scratch_shapes=[pltpu.VMEM((512, 2 * BG), jnp.bfloat16), pltpu.VMEM((G_TILES, 8, 128), jnp.float32)],
        compiler_params=pltpu.CompilerParams(vmem_limit_bytes=32 << 20),
    )(*chunks)


def a_cov_kernel(i0, i1, i2, i3, own, other, rows):
    c = lax.axis_index("c")
    r, k = grid_of(128)
    for zl in range(2):
        for which, out in ((c, own), (1 - c, other)):
            q = zl * 2 + which
            for s, ref in enumerate((i0, i1, i2, i3)):
                rows[s * 128:(s + 1) * 128, :] = ref[q]
            cov = gram(rows[...])
            corner = cov[128:, 128:]
            fold = jnp.where(r >= k, cov[:128, :128], corner)
            diag = jnp.sum(jnp.where(r == k, corner, 0.0), axis=0, keepdims=True)
            out[zl, 0:16] = cov[128:, :128].reshape(16, 8, 128)
            out[zl, 16:32] = fold.reshape(16, 8, 128)
            out[zl, 32] = jnp.broadcast_to(diag, (8, 128))
            out[zl, 33:] = jnp.zeros((A_TILES - 33, 8, 128), jnp.float32)


def a_cov(chunks):
    return pl.pallas_call(
        a_cov_kernel,
        out_shape=[jax.ShapeDtypeStruct((2, A_TILES, 8, 128), jnp.float32)] * 2,
        in_specs=[VMEM] * 4,
        out_specs=[VMEM] * 2,
        scratch_shapes=[pltpu.VMEM((512, BA), jnp.bfloat16)],
        compiler_params=pltpu.CompilerParams(vmem_limit_bytes=32 << 20),
    )(*chunks)


def reduce_pieces(value, axes):
    return jnp.sum(lax.all_to_all(value, axes, 0, 0, tiled=True), axis=0)


def gather_pieces(value, axes):
    size = lax.axis_size(axes)
    every = jnp.broadcast_to(value[None], (size, *value.shape))
    return lax.all_to_all(every, axes, 0, 0, tiled=True)


def split(value):
    high = value.astype(jnp.bfloat16)
    return high, (value - high.astype(jnp.float32)).astype(jnp.bfloat16)


def dot3(left, right):
    dot = functools.partial(jnp.dot, preferred_element_type=jnp.float32)
    return dot(left[0], right[0]) + (dot(left[0], right[1]) + dot(left[1], right[0]))


def newton(matrices, identity):
    n = identity.shape[0]
    state = []
    for matrix in matrices:
        trace = jnp.sum(matrix * identity)
        scaled = matrix / trace
        step = 2.0 * identity - scaled
        state.append((step / trace, dot3(split(scaled), split(step))))
    for _ in range(ITERS - 2):
        following = []
        for approx, product in state:
            both = dot3(split(jnp.concatenate([approx, product], axis=0)), split(2.0 * identity - product))
            following.append((both[:n], both[n:]))
        state = following
    return [dot3(split(approx), split(2.0 * identity - product)) for approx, product in state]


def a_side_kernel(tiles, running, g0, g1, g2, g3, left, *, token_total):
    r, k = grid_of(128)
    low = tiles[0:16].reshape(128, 128)
    fold = tiles[16:32].reshape(128, 128)
    diag = tiles[32][0:1]
    turned = fold.T
    top = jnp.where(r >= k, fold, turned)
    corner = jnp.where(r == k, jnp.broadcast_to(diag, (128, 128)), jnp.where(r < k, fold, turned))
    cov = jnp.concatenate([
        jnp.concatenate([top, low.T], axis=1), jnp.concatenate([low, corner], axis=1)
    ], axis=0)
    r, k = grid_of(BA)
    identity = jnp.where(r == k, 1.0, 0.0)
    mixed = factor_decay * running[0] + (1.0 - factor_decay) * cov / token_total
    inverse, = newton([mixed + damping * identity], identity)
    summed = (g0[...].astype(jnp.float32) + g1[...].astype(jnp.float32)) + (
        g2[...].astype(jnp.float32) + g3[...].astype(jnp.float32)
    )
    left[...] = dot3(split(inverse), split(summed))


def a_side(tiles, running, grads, token_total):
    return pl.pallas_call(
        functools.partial(a_side_kernel, token_total=token_total),
        out_shape=jax.ShapeDtypeStruct((BA, 2 * BG), jnp.float32),
        in_specs=[VMEM] * 6,
        out_specs=VMEM,
        compiler_params=pltpu.CompilerParams(vmem_limit_bytes=32 << 20),
        cost_estimate=pl.CostEstimate(flops=2_500_000_000, bytes_accessed=2_000_000, transcendentals=0),
    )(tiles, running, *grads)


def g_side_kernel(tiles, running, left, out, fold, wide, *, token_total):
    half = BG // 2
    for l in range(5):
        wide[:, l * 128:(l + 1) * 128] = tiles[l * 21:(l + 1) * 21].reshape(168, 128)
    fold[...] = jnp.zeros((BGP, BGP), jnp.float32)
    fold[0:half, 0:BG] = wide[0:half, 0:BG]
    fold[half:BG, 0:BG] = wide[0:half, BG:]
    diag = jnp.concatenate([wide[half:half + 1, 0:BG], jnp.zeros((1, BGP - BG), jnp.float32)], axis=1)
    r, k = grid_of(BGP)
    held = fold[...]
    turned = held.T
    first = jnp.where(r >= k, held, turned)
    second = jnp.where(r == k, jnp.broadcast_to(diag, (BGP, BGP)), jnp.where(r < k, held, turned))
    identity = jnp.where((r == k) & (r < BG), 1.0, 0.0)
    matrices = []
    for n, cov in enumerate((first, second)):
        fold[0:BG, 0:BG] = running[n]
        mixed = factor_decay * fold[...] + (1.0 - factor_decay) * cov / token_total
        matrices.append(mixed + damping * identity)
    inverse = newton(matrices, identity)
    for n in range(2):
        part = left[:, n * BG:(n + 1) * BG]
        done = dot3(split(part), split(inverse[n][:BG, :BG]))
        out[:, n * BG:(n + 1) * BG] = done.astype(jnp.bfloat16)


def g_side(tiles, running, left, token_total):
    return pl.pallas_call(
        functools.partial(g_side_kernel, token_total=token_total),
        out_shape=jax.ShapeDtypeStruct((BA, 2 * BG), jnp.bfloat16),
        in_specs=[VMEM] * 3,
        out_specs=VMEM,
        scratch_shapes=[pltpu.VMEM((BGP, BGP), jnp.float32), pltpu.VMEM((168, 2 * BG), jnp.float32)],
        compiler_params=pltpu.CompilerParams(vmem_limit_bytes=40 << 20),
        cost_estimate=pl.CostEstimate(flops=10_000_000_000, bytes_accessed=3_000_000, transcendentals=0),
    )(tiles, running, left)


def per_device(activations, out_grads, a_running, g_running, grad_partial):
    token_total = float(activations.shape[0] * 256)
    x, zl, c, y = (lax.axis_index(name) for name in ("x", "zl", "c", "y"))

    g_chunks = pack(out_grads, "x", 2 * BG)
    g_chunks, activations = lax.optimization_barrier((g_chunks, activations))
    g_in = send_round("x", g_chunks)
    a_in = send_round("y", pack(activations, "y", BA))
    grads = send_round("y", [
        lax.dynamic_slice_in_dim(grad_partial[0], lax.rem(y + s, 4) * BA, BA, 0) for s in range(4)
    ])
    g_in, a_in, grads = lax.optimization_barrier((g_in, a_in, grads))

    g_own, g_other = g_cov(g_in)
    a_own, a_other = a_cov(a_in)
    g_part = (g_own + swap_cores(g_other)).reshape(4, 4, 14, 8, 128)
    a_part = (a_own + swap_cores(a_other)).reshape(2, 4, 12, 8, 128)

    g_lines = send_round("y", [
        lax.dynamic_index_in_dim(g_part, lax.rem(y + s, 4), 1, keepdims=False) for s in range(4)
    ])
    a_lines = send_round("x", [
        lax.dynamic_index_in_dim(a_part, lax.rem(x + s, 4), 1, keepdims=False) for s in range(4)
    ])
    g_lines, a_lines = lax.optimization_barrier((g_lines, a_lines))
    g_line = (g_lines[0] + g_lines[1]) + (g_lines[2] + g_lines[3])
    a_line = (a_lines[0] + a_lines[1]) + (a_lines[2] + a_lines[3])

    both = jnp.concatenate([
        g_line.reshape(8, 56, 128),
        jnp.swapaxes(a_line.reshape(2, 4, 24, 128), 0, 1).reshape(8, 24, 128),
    ], axis=1)
    pieces = reduce_pieces(both, ("zh", "zl"))
    a_tiles = gather_pieces(pieces[56:], ("x", "zh")).reshape(A_TILES, 8, 128)
    g_piece, a_tiles = lax.optimization_barrier((pieces[:56], a_tiles))
    g_tiles = gather_pieces(g_piece, ("c", "y", "zl")).reshape(G_TILES, 8, 128)

    a_previous = lax.dynamic_slice_in_dim(a_running, (zl * 2 + c) * 4 + y, 1, 0)
    left = a_side(a_tiles, a_previous, grads, token_total)
    rows = g_side(g_tiles, g_running, left, token_total)

    out = jnp.zeros((4, BA, 2 * BG), jnp.bfloat16)
    for shift, got in enumerate(send_round("y", [rows] * 4)):
        out = lax.dynamic_update_slice_in_dim(out, got[None], lax.rem(y + 4 - shift, 4), 0)
    return out.reshape(4 * BA, 2 * BG)


def solution(mesh):
    fine = Mesh(mesh.devices.reshape(4, 4, 2, 2, 4), ("zh", "x", "zl", "c", "y"))
    tokens = P(("zh", "x", "zl", "c", "y"), None)
    placed = (tokens, tokens, P(), P(("zh", "x"), None, None), P("y", ("zl", "c"), ("zh", "x")))
    return jax.shard_map(
        per_device,
        mesh=fine,
        in_specs=placed,
        out_specs=P(("zl", "c"), ("zh", "x")),
        check_vma=False,
    )
```

```python
import functools

import jax
import jax.numpy as jnp
from jax import lax
from jax.experimental import pallas as pl
from jax.experimental.pallas import tpu as pltpu
from jax.sharding import Mesh, PartitionSpec as P

BA = 256
BG = 320
BGP = 384
ITERS = 8
G_TILES = 56
A_TILES = 48

factor_decay = 0.9
damping = 0.1

VMEM = pl.BlockSpec(memory_space=pltpu.VMEM)


def swap_cores(value):
    return lax.ppermute(value, "c", [(0, 1), (1, 0)])


def send_round(axis, chunks):
    size = lax.axis_size(axis)
    return [chunks[0]] + [
        lax.ppermute(chunks[s], axis, [(i, (i + s) % size) for i in range(size)])
        for s in range(1, size)
    ]


def pack_kernel(axis, width, src, *rest):
    outs, sem = rest[:4], rest[4]
    here = lax.axis_index(axis)
    copies = []
    for s in (1, 3, 2, 0):
        peer = lax.rem(here + s, 4)
        for q in range(4):
            start = pl.multiple_of((q * 4 + peer) * width, 128)
            copies.append(pltpu.make_async_copy(
                src.at[:, pl.ds(start, width)], outs[s].at[q], sem.at[s * 4 + q]
            ))
    for copy in copies:
        copy.start()
    for copy in copies:
        copy.wait()


def pack(samples, axis, width):
    piece = jax.ShapeDtypeStruct((4, samples.shape[0], width), samples.dtype)
    return pl.pallas_call(
        functools.partial(pack_kernel, axis, width),
        out_shape=[piece] * 4,
        in_specs=[pl.BlockSpec(memory_space=pl.ANY)],
        out_specs=[VMEM] * 4,
        scratch_shapes=[pltpu.SemaphoreType.DMA((16,))],
    )(samples)


def gram(v):
    return lax.dot_general(v, v, (((0,), (0,)), ((), ())), preferred_element_type=jnp.float32)


def grid_of(n):
    return (lax.broadcasted_iota(jnp.int32, (n, n), 0), lax.broadcasted_iota(jnp.int32, (n, n), 1))


def fold_block(cov, tiles, n):
    r, k = grid_of(128)
    corner = cov[128:256, 128:256]
    fold = jnp.where(r >= k, cov[0:128, 0:128], corner)
    diag = jnp.sum(jnp.where(r == k, corner, 0.0), axis=0, keepdims=True)
    tiles[n, 0:16] = fold.reshape(16, 8, 128)
    tiles[n, 16:32] = cov[128:256, 0:128].reshape(16, 8, 128)
    tiles[n, 32:40] = cov[256:BG, 0:128].reshape(8, 8, 128)
    tiles[n, 40:48] = cov[256:BG, 128:256].reshape(8, 8, 128)
    beside = jnp.concatenate([
        jnp.broadcast_to(diag[:, 0:64], (8, 64)),
        jnp.broadcast_to(diag[:, 64:128], (8, 64)),
        jnp.zeros((48, 64), jnp.float32),
    ], axis=0)
    tiles[n, 48:56] = jnp.concatenate([cov[256:BG, 256:BG], beside], axis=1).reshape(8, 8, 128)


def g_cov_kernel(i0, i1, i2, i3, own, other, rows, tiles):
    c = lax.axis_index("c")
    for s, ref in enumerate((i0, i1, i2, i3)):
        rows[s * 128:(s + 1) * 128, :] = ref[0]
    fold_block(gram(rows[:, 0:BGP]), tiles, 0)
    fold_block(gram(rows[:, 2 * BG - BGP:2 * BG])[BGP - BG:, BGP - BG:], tiles, 1)
    own[0] = tiles[c]
    other[0] = tiles[1 - c]


def g_cov(chunks):
    spec = pl.BlockSpec((1, 128, 2 * BG), lambda q: (q, 0, 0))
    out = pl.BlockSpec((1, 56, 8, 128), lambda q: (q, 0, 0, 0))
    return pl.pallas_call(
        g_cov_kernel,
        grid=(4,),
        out_shape=[jax.ShapeDtypeStruct((4, 56, 8, 128), jnp.float32)] * 2,
        in_specs=[spec] * 4,
        out_specs=[out] * 2,
        scratch_shapes=[pltpu.VMEM((512, 2 * BG), jnp.bfloat16), pltpu.VMEM((2, G_TILES, 8, 128), jnp.float32)],
        compiler_params=pltpu.CompilerParams(vmem_limit_bytes=32 << 20),
    )(*chunks)


def a_cov_kernel(i0, i1, i2, i3, own, other, rows):
    c = lax.axis_index("c")
    r, k = grid_of(128)
    for zl in range(2):
        for which, out in ((c, own), (1 - c, other)):
            q = zl * 2 + which
            for s, ref in enumerate((i0, i1, i2, i3)):
                rows[s * 128:(s + 1) * 128, :] = ref[q]
            cov = gram(rows[...])
            corner = cov[128:, 128:]
            fold = jnp.where(r >= k, cov[:128, :128], corner)
            diag = jnp.sum(jnp.where(r == k, corner, 0.0), axis=0, keepdims=True)
            out[zl, 0:16] = cov[128:, :128].reshape(16, 8, 128)
            out[zl, 16:32] = fold.reshape(16, 8, 128)
            out[zl, 32] = jnp.broadcast_to(diag, (8, 128))
            out[zl, 33:] = jnp.zeros((A_TILES - 33, 8, 128), jnp.float32)


def a_cov(chunks):
    return pl.pallas_call(
        a_cov_kernel,
        out_shape=[jax.ShapeDtypeStruct((2, A_TILES, 8, 128), jnp.float32)] * 2,
        in_specs=[VMEM] * 4,
        out_specs=[VMEM] * 2,
        scratch_shapes=[pltpu.VMEM((512, BA), jnp.bfloat16)],
        compiler_params=pltpu.CompilerParams(vmem_limit_bytes=32 << 20),
    )(*chunks)


def reduce_pieces(value, axes):
    return jnp.sum(lax.all_to_all(value, axes, 0, 0, tiled=True), axis=0)


def split(value):
    high = value.astype(jnp.bfloat16)
    return high, (value - high.astype(jnp.float32)).astype(jnp.bfloat16)


def dot3(left, right):
    dot = functools.partial(jnp.dot, preferred_element_type=jnp.float32)
    return dot(left[0], right[0]) + (dot(left[0], right[1]) + dot(left[1], right[0]))


def three(value):
    high, low = split(value)
    return high, high, low


def newton_even(matrix, identity, lhs, rhs):
    n = identity.shape[0]

    def put(approx, product):
        for i, part in enumerate(three(approx)):
            lhs[0:n, i * n:(i + 1) * n] = part
        for i, part in enumerate(three(product)):
            lhs[n:2 * n, i * n:(i + 1) * n] = part
        high, low = split(2.0 * identity - product)
        rhs[0:n], rhs[n:2 * n], rhs[2 * n:3 * n] = high, low, high

    trace = jnp.sum(matrix * identity)
    put(identity / trace, matrix / trace)

    def step(_, carry):
        both = jnp.dot(lhs[...], rhs[...], preferred_element_type=jnp.float32)
        put(both[:n], both[n:])
        return carry

    lax.fori_loop(0, ITERS - 1, step, 0)
    return jnp.dot(lhs[0:n], rhs[...], preferred_element_type=jnp.float32)


def a_side_kernel(got, running, g0, g1, g2, g3, keep, send, tiles, lhs, rhs, *, token_total):
    c, x = lax.axis_index("c"), lax.axis_index("x")
    for s in range(4):
        tiles[pl.ds(lax.rem(x + 4 - s, 4) * 12, 12)] = got[s]
    r, k = grid_of(128)
    low = tiles[0:16].reshape(128, 128)
    fold = tiles[16:32].reshape(128, 128)
    diag = tiles[32][0:1]
    turned = fold.T
    top = jnp.where(r >= k, fold, turned)
    corner = jnp.where(r == k, jnp.broadcast_to(diag, (128, 128)), jnp.where(r < k, fold, turned))
    cov = jnp.concatenate([
        jnp.concatenate([top, low.T], axis=1), jnp.concatenate([low, corner], axis=1)
    ], axis=0)
    r, k = grid_of(BA)
    identity = jnp.where(r == k, 1.0, 0.0)
    mixed = factor_decay * running[0] + (1.0 - factor_decay) * cov / token_total
    inverse = newton_even(mixed + damping * identity, identity, lhs, rhs)
    summed = (g0[...].astype(jnp.float32) + g1[...].astype(jnp.float32)) + (
        g2[...].astype(jnp.float32) + g3[...].astype(jnp.float32)
    )
    left = dot3(split(inverse), split(summed))
    keep[...] = jnp.where(c == 0, left[:, 0:BG], left[:, BG:])
    send[...] = jnp.where(c == 0, left[:, BG:], left[:, 0:BG])


def a_side(tiles, running, grads, token_total):
    return pl.pallas_call(
        functools.partial(a_side_kernel, token_total=token_total),
        out_shape=[jax.ShapeDtypeStruct((BA, BG), jnp.float32)] * 2,
        in_specs=[VMEM] * 6,
        out_specs=[VMEM] * 2,
        scratch_shapes=[
            pltpu.VMEM((A_TILES, 8, 128), jnp.float32),
            pltpu.VMEM((2 * BA, 3 * BA), jnp.bfloat16), pltpu.VMEM((3 * BA, BA), jnp.bfloat16)
        ],
        compiler_params=pltpu.CompilerParams(vmem_limit_bytes=32 << 20),
        cost_estimate=pl.CostEstimate(flops=2_500_000_000, bytes_accessed=2_000_000, transcendentals=0),
    )(tiles, running, *grads)


def turned_tail(main):
    tail = main[256:BG]
    return jnp.concatenate([tail, jnp.zeros_like(tail)], axis=0).T


def unfold_block(tiles):
    r, k = grid_of(128)
    fold = tiles[0:16].reshape(128, 128)
    low = tiles[16:32].reshape(128, 128)
    last = tiles[48:56].reshape(64, 128)
    diag = jnp.concatenate([last[0:1, 64:128], last[8:9, 64:128]], axis=1)
    turned = fold.T
    first = jnp.where(r >= k, fold, turned)
    second = jnp.where(r == k, jnp.broadcast_to(diag, (128, 128)), jnp.where(r < k, fold, turned))
    bottom = [tiles[32:40].reshape(64, 128), tiles[40:48].reshape(64, 128)]
    main = jnp.concatenate([
        jnp.concatenate([first, low.T], axis=1),
        jnp.concatenate([low, second], axis=1),
        jnp.concatenate(bottom, axis=1),
    ], axis=0)
    empty = jnp.zeros((64, 128), jnp.float32)
    r, k = lax.broadcasted_iota(jnp.int32, (64, 128), 0), lax.broadcasted_iota(jnp.int32, (64, 128), 1)
    tail = jnp.concatenate([jnp.concatenate([part, empty], axis=0).T for part in bottom]
                           + [jnp.where(k < 64, last, 0.0)], axis=0)
    return main, tail


def g_put(lhs, rhs_main, rhs_tail, ident, approx, product):
    for row, (main, tail) in ((0, approx), (BG, product)):
        for i, (part, edge) in enumerate(zip(three(main), three(tail))):
            lhs[row:row + BG, i * BGP:i * BGP + 256] = part
            lhs[row:row + BG, i * BGP + 256:(i + 1) * BGP] = edge
    for rhs, same, value in ((rhs_main, ident[0], product[0]), (rhs_tail, ident[1], product[1])):
        high, low = split(2.0 * same - value)
        rhs[0:BG] = high
        rhs[BGP:BGP + BG] = low
        rhs[2 * BGP:2 * BGP + BG] = high


def g_side_kernel(
    got, running, left_own, left_sibling, own, sibling, tiles, lhs, rhs_main, rhs_tail, *, token_total
):
    c, y, zl = (lax.axis_index(name) for name in ("c", "y", "zl"))
    for z, near in enumerate((zl, 1 - zl)):
        for s in range(4):
            tiles[pl.ds(lax.rem(y + 4 - s, 4) * 14 + near * 7, 7)] = got[z, s]
    new_sum = unfold_block(tiles)
    previous = running[c, :, 0:256], jnp.concatenate(
        [running[c, :, 256:BG], jnp.zeros((BG, 64), jnp.float32)], axis=1
    )
    r, k = lax.broadcasted_iota(jnp.int32, (BG, 256), 0), lax.broadcasted_iota(jnp.int32, (BG, 256), 1)
    ident = [jnp.where(r == k, 1.0, 0.0)]
    r, k = lax.broadcasted_iota(jnp.int32, (BG, 128), 0), lax.broadcasted_iota(jnp.int32, (BG, 128), 1)
    ident.append(jnp.where(r == k + 256, 1.0, 0.0))
    matrix = [
        (factor_decay * before + (1.0 - factor_decay) * cov / token_total) + damping * same
        for before, cov, same in zip(previous, new_sum, ident)
    ]
    trace = sum(jnp.sum(part * same) for part, same in zip(matrix, ident))
    rhs_main[...] = jnp.zeros(rhs_main.shape, jnp.bfloat16)
    rhs_tail[...] = jnp.zeros(rhs_tail.shape, jnp.bfloat16)
    put = functools.partial(g_put, lhs, rhs_main, rhs_tail, ident)
    put([same / trace for same in ident], [part / trace for part in matrix])

    def product(rows):
        main = jnp.dot(lhs[0:rows], rhs_main[...], preferred_element_type=jnp.float32)
        corners = [
            jnp.dot(lhs[row + 256:row + BG], rhs_tail[...], preferred_element_type=jnp.float32)
            for row in range(0, rows, BG)
        ]
        return [
            (main[row:row + BG], jnp.concatenate([turned_tail(main[row:row + BG]), corner], axis=0))
            for row, corner in zip(range(0, rows, BG), corners)
        ]

    def step(_, carry):
        put(*product(2 * BG))
        return carry

    lax.fori_loop(0, ITERS - 1, step, 0)
    (main, tail), = product(BG)
    inverse = split(jnp.concatenate([main, tail], axis=1))
    for left, out in ((left_sibling, sibling), (left_own, own)):
        out[...] = dot3(split(left[...]), inverse)[:, 0:BG].astype(jnp.bfloat16)


def g_side(got, running, left_own, left_sibling, token_total):
    return pl.pallas_call(
        functools.partial(g_side_kernel, token_total=token_total),
        out_shape=[jax.ShapeDtypeStruct((BA, BG), jnp.bfloat16)] * 2,
        in_specs=[VMEM] * 4,
        out_specs=[VMEM] * 2,
        scratch_shapes=[
            pltpu.VMEM((G_TILES, 8, 128), jnp.float32),
            pltpu.VMEM((2 * BG, 3 * BGP), jnp.bfloat16),
            pltpu.VMEM((3 * BGP, 256), jnp.bfloat16),
            pltpu.VMEM((3 * BGP, 128), jnp.bfloat16),
        ],
        compiler_params=pltpu.CompilerParams(vmem_limit_bytes=40 << 20),
        cost_estimate=pl.CostEstimate(flops=6_000_000_000, bytes_accessed=3_000_000, transcendentals=0),
    )(got, running, left_own, left_sibling)


def per_device(activations, out_grads, a_running, g_running, grad_partial):
    token_total = float(activations.shape[0] * 256)
    x, zl, c, y = (lax.axis_index(name) for name in ("x", "zl", "c", "y"))

    g_chunks = pack(out_grads, "x", 2 * BG)
    g_chunks, activations = lax.optimization_barrier((g_chunks, activations))
    g_in = send_round("x", g_chunks)
    a_in = send_round("y", pack(activations, "y", BA))
    g_in, a_in = lax.optimization_barrier((g_in, a_in))

    g_own, g_other = g_cov(g_in)
    a_own, a_other = a_cov(a_in)
    g_part = (g_own + swap_cores(g_other)).reshape(4, 4, 14, 8, 128)
    a_part = (a_own + swap_cores(a_other)).reshape(2, 4, 12, 8, 128)

    g_lines = send_round("y", [
        lax.dynamic_index_in_dim(g_part, lax.rem(y + s, 4), 1, keepdims=False) for s in range(4)
    ])
    a_lines = send_round("x", [
        lax.dynamic_index_in_dim(a_part, lax.rem(x + s, 4), 1, keepdims=False) for s in range(4)
    ])
    g_lines, a_lines, grad_partial = lax.optimization_barrier((g_lines, a_lines, grad_partial))
    grads = send_round("y", [
        lax.dynamic_slice_in_dim(grad_partial[0], lax.rem(y + s, 4) * BA, BA, 0) for s in range(4)
    ])
    g_line = (g_lines[0] + g_lines[1]) + (g_lines[2] + g_lines[3])
    a_line = (a_lines[0] + a_lines[1]) + (a_lines[2] + a_lines[3])

    both = jnp.concatenate([
        g_line.reshape(8, 56, 128),
        jnp.broadcast_to(a_line.reshape(1, 2, 96, 128), (4, 2, 96, 128)).reshape(8, 96, 128),
    ], axis=1)
    pieces = reduce_pieces(both, ("zh", "zl"))
    pieces, grads = lax.optimization_barrier((pieces, grads))

    g_rows = jnp.stack(send_round("y", [pieces[:56]] * 4))
    a_tiles = jnp.stack(send_round("x", [pieces[56:]] * 4)).reshape(4, 12, 8, 128)
    g_tiles = jnp.stack([g_rows, lax.ppermute(g_rows, "zl", [(0, 1), (1, 0)])]).reshape(2, 4, 7, 8, 128)

    a_previous = lax.dynamic_slice_in_dim(a_running, (zl * 2 + c) * 4 + y, 1, 0)
    left, left_send = a_side(a_tiles, a_previous, grads, token_total)
    own, sibling = g_side(g_tiles, g_running, left, swap_cores(left_send), token_total)
    got = swap_cores(sibling)
    rows = jnp.concatenate([jnp.where(c == 0, own, got), jnp.where(c == 0, got, own)], axis=1)

    out = jnp.zeros((4, BA, 2 * BG), jnp.bfloat16)
    for shift, got in enumerate(send_round("y", [rows] * 4)):
        out = lax.dynamic_update_slice_in_dim(out, got[None], lax.rem(y + 4 - shift, 4), 0)
    return out.reshape(4 * BA, 2 * BG)


def solution(mesh):
    fine = Mesh(mesh.devices.reshape(4, 4, 2, 2, 4), ("zh", "x", "zl", "c", "y"))
    tokens = P(("zh", "x", "zl", "c", "y"), None)
    placed = (tokens, tokens, P(), P(("zh", "x"), None, None), P("y", ("zl", "c"), ("zh", "x")))
    return jax.shard_map(
        per_device,
        mesh=fine,
        in_specs=placed,
        out_specs=P(("zl", "c"), ("zh", "x")),
        check_vma=False,
    )
```

```python
import functools

import jax
import jax.numpy as jnp
from jax import lax
from jax.experimental import pallas as pl
from jax.experimental.pallas import tpu as pltpu
from jax.sharding import Mesh, PartitionSpec as P

BA = 256
BG = 320
BGP = 384
ITERS = 8
G_TILES = 56
A_TILES = 36

factor_decay = 0.9
damping = 0.1

VMEM = pl.BlockSpec(memory_space=pltpu.VMEM)


def swap_cores(value):
    return lax.ppermute(value, "c", [(0, 1), (1, 0)])


def send(value, axis, s):
    return lax.ppermute(value, axis, [(i, (i + s) % 4) for i in range(4)])


def swap_pair(value):
    return lax.ppermute(value, "zl", [(0, 1), (1, 0)])


def send_round(axis, chunks):
    return [chunks[0]] + [send(chunks[s], axis, s) for s in range(1, 4)]


def run_copies(pairs, sem):
    copies = [pltpu.make_async_copy(src, dst, sem.at[i]) for i, (src, dst) in enumerate(pairs)]
    for copy in copies:
        copy.start()
    for copy in copies:
        copy.wait()


def x_chunk(src, s, out):
    peer = lax.rem(lax.axis_index("x") + s, 4)
    for q in range(4):
        start = pl.multiple_of((q * 4 + peer) * 2 * BG, 128)
        yield src.at[:, pl.ds(start, 2 * BG)], out.at[q]


def y_chunk(samples, grads, s, out):
    peer = lax.rem(lax.axis_index("y") + s, 4)
    for q in range(4):
        start = pl.multiple_of((q * 4 + peer) * BA, 128)
        yield samples.at[:, pl.ds(start, BA)], out.at[:, pl.ds(q * BA, BA)]
    for h in range(2):
        start = pl.multiple_of(peer * BA + h * 128, 128)
        yield grads.at[0, pl.ds(start, 128), :], out.at[:, pl.ds(4 * BA + h * 2 * BG, 2 * BG)]


def near_x_kernel(src, out1, out3, sem):
    run_copies([pair for s, out in ((1, out1), (3, out3)) for pair in x_chunk(src, s, out)], sem)


def near_y_kernel(samples, grads, out1, out3, sem):
    run_copies([pair for s, out in ((1, out1), (3, out3)) for pair in y_chunk(samples, grads, s, out)], sem)


def rest_kernel(src, samples, grads, running, far_x, far_y, own_x, own_y, previous, sem):
    zl, c, y = (lax.axis_index(name) for name in ("zl", "c", "y"))
    run_copies([
        *x_chunk(src, 2, far_x), *y_chunk(samples, grads, 2, far_y),
        *x_chunk(src, 0, own_x), *y_chunk(samples, grads, 0, own_y),
        (running.at[(zl * 2 + c) * 4 + y], previous),
    ], sem)


X_CHUNK = jax.ShapeDtypeStruct((4, 128, 2 * BG), jnp.bfloat16)
Y_CHUNK = jax.ShapeDtypeStruct((128, 4 * BA + 4 * BG), jnp.bfloat16)
PREVIOUS = jax.ShapeDtypeStruct((BA, BA), jnp.float32)


def pack(kernel, count, out_shape, *args):
    return pl.pallas_call(
        kernel,
        out_shape=out_shape,
        in_specs=[pl.BlockSpec(memory_space=pl.ANY)] * len(args),
        out_specs=[VMEM] * len(out_shape),
        scratch_shapes=[pltpu.SemaphoreType.DMA((count,))],
    )(*args)


def gram(v):
    return lax.dot_general(v, v, (((0,), (0,)), ((), ())), preferred_element_type=jnp.float32)


def grid_of(n):
    return (lax.broadcasted_iota(jnp.int32, (n, n), 0), lax.broadcasted_iota(jnp.int32, (n, n), 1))


def fold_block(cov, tiles, n):
    r, k = grid_of(128)
    corner = cov[128:256, 128:256]
    fold = jnp.where(r >= k, cov[0:128, 0:128], corner)
    diag = jnp.sum(jnp.where(r == k, corner, 0.0), axis=0, keepdims=True)
    tiles[n, 0:16] = fold.reshape(16, 8, 128)
    tiles[n, 16:32] = cov[128:256, 0:128].reshape(16, 8, 128)
    tiles[n, 32:40] = cov[256:BG, 0:128].reshape(8, 8, 128)
    tiles[n, 40:48] = cov[256:BG, 128:256].reshape(8, 8, 128)
    beside = jnp.concatenate([
        jnp.broadcast_to(diag[:, 0:64], (8, 64)),
        jnp.broadcast_to(diag[:, 64:128], (8, 64)),
        jnp.zeros((48, 64), jnp.float32),
    ], axis=0)
    tiles[n, 48:56] = jnp.concatenate([cov[256:BG, 256:BG], beside], axis=1).reshape(8, 8, 128)


def g_cov_kernel(i0, i1, i2, i3, own, other, rows, tiles):
    c = lax.axis_index("c")
    for s, ref in enumerate((i0, i1, i2, i3)):
        rows[s * 128:(s + 1) * 128, :] = ref[0]
    fold_block(gram(rows[:, 0:BGP]), tiles, 0)
    fold_block(gram(rows[:, 2 * BG - BGP:2 * BG])[BGP - BG:, BGP - BG:], tiles, 1)
    own[0] = tiles[c]
    other[0] = tiles[1 - c]


def g_cov(chunks):
    spec = pl.BlockSpec((1, 128, 2 * BG), lambda q: (q, 0, 0))
    out = pl.BlockSpec((1, 56, 8, 128), lambda q: (q, 0, 0, 0))
    return pl.pallas_call(
        g_cov_kernel,
        grid=(4,),
        out_shape=[jax.ShapeDtypeStruct((4, 56, 8, 128), jnp.float32)] * 2,
        in_specs=[spec] * 4,
        out_specs=[out] * 2,
        scratch_shapes=[pltpu.VMEM((512, 2 * BG), jnp.bfloat16), pltpu.VMEM((2, G_TILES, 8, 128), jnp.float32)],
        compiler_params=pltpu.CompilerParams(vmem_limit_bytes=16 << 20),
    )(*chunks)


def a_cov_kernel(i0, i1, i2, i3, own, other, rows, tiles):
    c = lax.axis_index("c")
    r, k = grid_of(128)
    for zl in range(2):
        for core in range(2):
            q = zl * 2 + core
            for s, ref in enumerate((i0, i1, i2, i3)):
                rows[s * 128:(s + 1) * 128, :] = ref[:, q * BA:(q + 1) * BA]
            cov = gram(rows[...])
            corner = cov[128:, 128:]
            fold = jnp.where(r >= k, cov[:128, :128], corner)
            diag = jnp.sum(jnp.where(r == k, corner, 0.0), axis=0, keepdims=True)
            tiles[core, 0:16] = cov[128:, :128].reshape(16, 8, 128)
            tiles[core, 16:32] = fold.reshape(16, 8, 128)
            tiles[core, 32] = jnp.broadcast_to(diag, (8, 128))
            tiles[core, 33:] = jnp.zeros((A_TILES - 33, 8, 128), jnp.float32)
        own[zl] = tiles[c]
        other[zl] = tiles[1 - c]


def a_cov(chunks):
    return pl.pallas_call(
        a_cov_kernel,
        out_shape=[jax.ShapeDtypeStruct((2, A_TILES, 8, 128), jnp.float32)] * 2,
        in_specs=[VMEM] * 4,
        out_specs=[VMEM] * 2,
        scratch_shapes=[pltpu.VMEM((512, BA), jnp.bfloat16), pltpu.VMEM((2, A_TILES, 8, 128), jnp.float32)],
        compiler_params=pltpu.CompilerParams(vmem_limit_bytes=16 << 20),
    )(*chunks)


def tile_shape(*dims):
    return jax.ShapeDtypeStruct((*dims, 8, 128), jnp.float32)


def local(kernel, out_shape, *args):
    return pl.pallas_call(
        kernel,
        out_shape=out_shape,
        in_specs=[VMEM] * len(args),
        out_specs=jax.tree.map(lambda _: VMEM, out_shape),
        compiler_params=pltpu.CompilerParams(vmem_limit_bytes=16 << 20),
    )(*args)


def cores_kernel(g_own, g_got, a_own, a_got, *outs):
    x, y = lax.axis_index("x"), lax.axis_index("y")
    for s in range(4):
        place = pl.ds(lax.rem(y + s, 4) * 14, 14)
        outs[s][...] = g_own[:, place] + g_got[:, place]
        place = pl.ds(lax.rem(x + s, 4) * 9, 9)
        outs[4 + s][...] = a_own[:, place] + a_got[:, place]


def lines_kernel(g0, g1, g2, g3, a0, a1, a2, a3, keep, turn):
    zl = lax.axis_index("zl")
    for out, side in ((keep, zl), (turn, 1 - zl)):
        for q in range(4):
            place = pl.ds(side * 7, 7)
            out[q * 7:q * 7 + 7] = (g0[q, place] + g1[q, place]) + (g2[q, place] + g3[q, place])
        out[28:] = (a0[side] + a1[side]) + (a2[side] + a3[side])


def pairs_kernel(keep, got, *outs):
    zh = lax.axis_index("zh")
    a_sum = keep[28:] + got[28:]
    for s in range(4):
        place = pl.ds(lax.rem(zh + s, 4) * 7, 7)
        outs[s][0:7] = keep[place] + got[place]
        outs[s][7:] = a_sum


def pieces_kernel(p0, p1, p2, p3, g_piece, a_piece):
    g_piece[...] = (p0[0:7] + p1[0:7]) + (p2[0:7] + p3[0:7])
    a_piece[...] = (p0[7:] + p1[7:]) + (p2[7:] + p3[7:])


def join_kernel(own, got, out):
    zl = lax.axis_index("zl")
    out[pl.ds(zl * 7, 7)] = own[...]
    out[pl.ds((1 - zl) * 7, 7)] = got[...]


def split(value):
    high = value.astype(jnp.bfloat16)
    return high, (value - high.astype(jnp.float32)).astype(jnp.bfloat16)


def dot3(left, right):
    dot = functools.partial(jnp.dot, preferred_element_type=jnp.float32)
    return dot(left[0], right[0]) + (dot(left[0], right[1]) + dot(left[1], right[0]))


def three(value):
    high, low = split(value)
    return high, high, low


def newton_even(matrix, identity, lhs, rhs):
    n = identity.shape[0]

    def put(approx, product):
        for i, part in enumerate(three(approx)):
            lhs[0:n, i * n:(i + 1) * n] = part
        for i, part in enumerate(three(product)):
            lhs[n:2 * n, i * n:(i + 1) * n] = part
        high, low = split(2.0 * identity - product)
        rhs[0:n], rhs[n:2 * n], rhs[2 * n:3 * n] = high, low, high

    trace = jnp.sum(matrix * identity)
    put(identity / trace, matrix / trace)

    def step(_, carry):
        both = jnp.dot(lhs[...], rhs[...], preferred_element_type=jnp.float32)
        put(both[:n], both[n:])
        return carry

    lax.fori_loop(0, ITERS - 1, step, 0)
    return jnp.dot(lhs[0:n], rhs[...], preferred_element_type=jnp.float32)


def a_side_kernel(p0, p1, p2, p3, running, g0, g1, g2, g3, left, tiles, lhs, rhs, *, token_total):
    x = lax.axis_index("x")
    for s, got in enumerate((p0, p1, p2, p3)):
        tiles[pl.ds(lax.rem(x + 4 - s, 4) * 9, 9)] = got[...]
    r, k = grid_of(128)
    low = tiles[0:16].reshape(128, 128)
    fold = tiles[16:32].reshape(128, 128)
    diag = tiles[32][0:1]
    turned = fold.T
    top = jnp.where(r >= k, fold, turned)
    corner = jnp.where(r == k, jnp.broadcast_to(diag, (128, 128)), jnp.where(r < k, fold, turned))
    cov = jnp.concatenate([
        jnp.concatenate([top, low.T], axis=1), jnp.concatenate([low, corner], axis=1)
    ], axis=0)
    r, k = grid_of(BA)
    identity = jnp.where(r == k, 1.0, 0.0)
    mixed = factor_decay * running[...] + (1.0 - factor_decay) * cov / token_total
    inverse = newton_even(mixed + damping * identity, identity, lhs, rhs)
    summed = []
    for h in range(2):
        begin = 4 * BA + h * 2 * BG
        g = [ref[:, begin:begin + 2 * BG].astype(jnp.float32) for ref in (g0, g1, g2, g3)]
        summed.append((g[0] + g[1]) + (g[2] + g[3]))
    summed = jnp.concatenate(summed, axis=0)
    done = dot3(split(inverse), split(summed))
    for n in range(2):
        left[n] = done[:, n * BG:(n + 1) * BG]


def a_side(pieces, running, grads, token_total):
    return pl.pallas_call(
        functools.partial(a_side_kernel, token_total=token_total),
        out_shape=jax.ShapeDtypeStruct((2, BA, BG), jnp.float32),
        in_specs=[VMEM] * 9,
        out_specs=VMEM,
        scratch_shapes=[
            pltpu.VMEM((A_TILES, 8, 128), jnp.float32),
            pltpu.VMEM((2 * BA, 3 * BA), jnp.bfloat16), pltpu.VMEM((3 * BA, BA), jnp.bfloat16)
        ],
        compiler_params=pltpu.CompilerParams(vmem_limit_bytes=16 << 20),
        cost_estimate=pl.CostEstimate(flops=2_500_000_000, bytes_accessed=2_000_000, transcendentals=0),
    )(*pieces, running, *grads)


def turned_tail(main):
    tail = main[256:BG]
    return jnp.concatenate([tail, jnp.zeros_like(tail)], axis=0).T


HALF = jax.ShapeDtypeStruct((128, 2 * BG), jnp.bfloat16)


def unfold_block(tiles):
    r, k = grid_of(128)
    fold = tiles[0:16].reshape(128, 128)
    low = tiles[16:32].reshape(128, 128)
    last = tiles[48:56].reshape(64, 128)
    diag = jnp.concatenate([last[0:1, 64:128], last[8:9, 64:128]], axis=1)
    turned = fold.T
    first = jnp.where(r >= k, fold, turned)
    second = jnp.where(r == k, jnp.broadcast_to(diag, (128, 128)), jnp.where(r < k, fold, turned))
    bottom = [tiles[32:40].reshape(64, 128), tiles[40:48].reshape(64, 128)]
    main = jnp.concatenate([
        jnp.concatenate([first, low.T], axis=1),
        jnp.concatenate([low, second], axis=1),
        jnp.concatenate(bottom, axis=1),
    ], axis=0)
    empty = jnp.zeros((64, 128), jnp.float32)
    r, k = lax.broadcasted_iota(jnp.int32, (64, 128), 0), lax.broadcasted_iota(jnp.int32, (64, 128), 1)
    tail = jnp.concatenate([jnp.concatenate([part, empty], axis=0).T for part in bottom]
                           + [jnp.where(k < 64, last, 0.0)], axis=0)
    return main, tail


def g_put(lhs, rhs_main, rhs_tail, ident, approx, product):
    for row, (main, tail) in ((0, approx), (BG, product)):
        for i, (part, edge) in enumerate(zip(three(main), three(tail))):
            lhs[row:row + BG, i * BGP:i * BGP + 256] = part
            lhs[row:row + BG, i * BGP + 256:(i + 1) * BGP] = edge
    for rhs, same, value in ((rhs_main, ident[0], product[0]), (rhs_tail, ident[1], product[1])):
        high, low = split(2.0 * same - value)
        rhs[0:BG] = high
        rhs[BGP:BGP + BG] = low
        rhs[2 * BGP:2 * BGP + BG] = high


def half_rows(left, inverse):
    done = dot3(split(left), (inverse[0], inverse[1]))[:, 0:BG].astype(jnp.bfloat16)
    return jnp.concatenate([done[0:128], done[128:BA]], axis=1)


def g_side_kernel(p0, p1, p2, p3, running, left, out, rows, tiles, lhs, rhs_main, rhs_tail, *, token_total):
    c, y = lax.axis_index("c"), lax.axis_index("y")
    for s, got in enumerate((p0, p1, p2, p3)):
        tiles[pl.ds(lax.rem(y + 4 - s, 4) * 14, 14)] = got[...]
    new_sum = unfold_block(tiles)
    previous = running[c, :, 0:256], jnp.concatenate(
        [running[c, :, 256:BG], jnp.zeros((BG, 64), jnp.float32)], axis=1
    )
    r, k = lax.broadcasted_iota(jnp.int32, (BG, 256), 0), lax.broadcasted_iota(jnp.int32, (BG, 256), 1)
    ident = [jnp.where(r == k, 1.0, 0.0)]
    r, k = lax.broadcasted_iota(jnp.int32, (BG, 128), 0), lax.broadcasted_iota(jnp.int32, (BG, 128), 1)
    ident.append(jnp.where(r == k + 256, 1.0, 0.0))
    matrix = [
        (factor_decay * before + (1.0 - factor_decay) * cov / token_total) + damping * same
        for before, cov, same in zip(previous, new_sum, ident)
    ]
    trace = sum(jnp.sum(part * same) for part, same in zip(matrix, ident))
    rhs_main[...] = jnp.zeros(rhs_main.shape, jnp.bfloat16)
    rhs_tail[...] = jnp.zeros(rhs_tail.shape, jnp.bfloat16)
    put = functools.partial(g_put, lhs, rhs_main, rhs_tail, ident)
    put([same / trace for same in ident], [part / trace for part in matrix])

    def product(rows):
        main = jnp.dot(lhs[0:rows], rhs_main[...], preferred_element_type=jnp.float32)
        corners = [
            jnp.dot(lhs[row + 256:row + BG], rhs_tail[...], preferred_element_type=jnp.float32)
            for row in range(0, rows, BG)
        ]
        return [
            (main[row:row + BG], jnp.concatenate([turned_tail(main[row:row + BG]), corner], axis=0))
            for row, corner in zip(range(0, rows, BG), corners)
        ]

    def step(_, carry):
        put(*product(2 * BG))
        return carry

    lax.fori_loop(0, ITERS - 1, step, 0)
    (main, tail), = product(BG)
    out[0], out[1] = split(jnp.concatenate([main, tail], axis=1))
    rows[...] = half_rows(left[c], out)


def g_side(pieces, running, left, token_total):
    return pl.pallas_call(
        functools.partial(g_side_kernel, token_total=token_total),
        out_shape=[jax.ShapeDtypeStruct((2, BG, BGP), jnp.bfloat16), HALF],
        in_specs=[VMEM] * 6,
        out_specs=[VMEM] * 2,
        scratch_shapes=[
            pltpu.VMEM((G_TILES, 8, 128), jnp.float32),
            pltpu.VMEM((2 * BG, 3 * BGP), jnp.bfloat16),
            pltpu.VMEM((3 * BGP, 256), jnp.bfloat16),
            pltpu.VMEM((3 * BGP, 128), jnp.bfloat16),
        ],
        compiler_params=pltpu.CompilerParams(vmem_limit_bytes=16 << 20),
        cost_estimate=pl.CostEstimate(flops=6_000_000_000, bytes_accessed=3_000_000, transcendentals=0),
    )(*pieces, running, left)


def apply_kernel(left, theirs, rows):
    rows[...] = half_rows(left[1 - lax.axis_index("c")], theirs)


def assemble_kernel(*refs):
    first, second, out = refs[:4], refs[4:8], refs[8]
    c, y = lax.axis_index("c"), lax.axis_index("y")
    for s in range(4):
        mine, theirs = first[s][...], second[s][...]
        halves = jnp.where(c == 0, mine, theirs), jnp.where(c == 0, theirs, mine)
        start = pl.multiple_of(lax.rem(y + 4 - s, 4) * BA, BA)
        for h in range(2):
            out[pl.ds(start + h * 128, 128), :] = jnp.concatenate(
                [half[:, h * BG:(h + 1) * BG] for half in halves], axis=1
            )


def per_device(activations, out_grads, a_running, g_running, grad_partial):
    token_total = float(activations.shape[0] * 256)
    y = lax.axis_index("y")

    near_x = pack(near_x_kernel, 8, [X_CHUNK] * 2, out_grads)
    near_x, activations = lax.optimization_barrier((near_x, activations))
    near_y = pack(near_y_kernel, 12, [Y_CHUNK] * 2, activations, grad_partial)
    near_y, out_grads = lax.optimization_barrier((near_y, out_grads))
    far_x, far_y, own_x, own_y, a_previous = pack(
        rest_kernel, 21, [X_CHUNK, Y_CHUNK, X_CHUNK, Y_CHUNK, PREVIOUS],
        out_grads, activations, grad_partial, a_running,
    )
    g_in = [send(near_x[0], "x", 1), send(near_x[1], "x", 3)]
    y_in = [send(near_y[0], "y", 1), send(near_y[1], "y", 3)]
    g_in, y_in, far_x, far_y = lax.optimization_barrier((g_in, y_in, far_x, far_y))
    g_in = [own_x, *g_in, send(far_x, "x", 2)]
    y_in = [own_y, *y_in, send(far_y, "y", 2)]
    g_in, y_in = lax.optimization_barrier((g_in, y_in))

    g_own, g_other = g_cov(g_in)
    a_own, a_other = a_cov(y_in)
    cut = local(
        cores_kernel, [tile_shape(4, 14)] * 4 + [tile_shape(2, 9)] * 4,
        g_own, swap_cores(g_other), a_own, swap_cores(a_other),
    )
    lines = lax.optimization_barrier(send_round("y", cut[:4]) + send_round("x", cut[4:]))
    keep, turn = local(lines_kernel, [tile_shape(37)] * 2, *lines)
    cut = local(pairs_kernel, [tile_shape(16)] * 4, keep, swap_pair(turn))
    g_piece, a_piece = local(pieces_kernel, [tile_shape(7), tile_shape(9)], *send_round("zh", cut))

    a_pieces = send_round("x", [a_piece] * 4)
    g_pair = local(join_kernel, tile_shape(14), g_piece, swap_pair(g_piece))
    g_pieces = send_round("y", [g_pair] * 4)
    left = a_side(a_pieces, a_previous, y_in, token_total)
    g_pieces, left = lax.optimization_barrier((g_pieces, left))
    inverse, first = g_side(g_pieces, g_running, left, token_total)
    second = local(apply_kernel, HALF, left, swap_cores(inverse))
    parts = send_round("y", [first] * 4) + send_round("y", [second] * 4)
    return local(assemble_kernel, jax.ShapeDtypeStruct((4 * BA, 2 * BG), jnp.bfloat16), *parts)


def solution(mesh):
    fine = Mesh(mesh.devices.reshape(4, 4, 2, 2, 4), ("zh", "x", "zl", "c", "y"))
    tokens = P(("zh", "x", "zl", "c", "y"), None)
    placed = (tokens, tokens, P(), P(("zh", "x"), None, None), P("y", ("zl", "c"), ("zh", "x")))
    return jax.shard_map(
        per_device,
        mesh=fine,
        in_specs=placed,
        out_specs=P(("zl", "c"), ("zh", "x")),
        check_vma=False,
    )
```

```python
import functools

import jax
import jax.numpy as jnp
from jax import lax
from jax.experimental import pallas as pl
from jax.experimental.pallas import tpu as pltpu
from jax.sharding import Mesh, PartitionSpec as P

BA = 256
BG = 320
BGP = 384
ITERS = 8
G_TILES = 56
A_TILES = 36

factor_decay = 0.9
damping = 0.1

VMEM = pl.BlockSpec(memory_space=pltpu.VMEM)


def swap_cores(value):
    return lax.ppermute(value, "c", [(0, 1), (1, 0)])


def send(value, axis, s):
    return lax.ppermute(value, axis, [(i, (i + s) % 4) for i in range(4)])


def swap_pair(value):
    return lax.ppermute(value, "zl", [(0, 1), (1, 0)])


def send_round(axis, chunks):
    return [chunks[0]] + [send(chunks[s], axis, s) for s in range(1, 4)]


def run_copies(pairs, sem):
    copies = [pltpu.make_async_copy(src, dst, sem.at[i]) for i, (src, dst) in enumerate(pairs)]
    for copy in copies:
        copy.start()
    for copy in copies:
        copy.wait()


def x_chunk(src, s, out):
    peer = lax.rem(lax.axis_index("x") + s, 4)
    for q in range(4):
        start = pl.multiple_of((q * 4 + peer) * 2 * BG, 128)
        yield src.at[:, pl.ds(start, 2 * BG)], out.at[q]


def y_chunk(samples, grads, s, out):
    peer = lax.rem(lax.axis_index("y") + s, 4)
    for q in range(4):
        start = pl.multiple_of((q * 4 + peer) * BA, 128)
        yield samples.at[:, pl.ds(start, BA)], out.at[:, pl.ds(q * BA, BA)]
    for h in range(2):
        start = pl.multiple_of(peer * BA + h * 128, 128)
        yield grads.at[0, pl.ds(start, 128), :], out.at[:, pl.ds(4 * BA + h * 2 * BG, 2 * BG)]


def near_x_kernel(src, out1, out3, sem):
    run_copies([pair for s, out in ((1, out1), (3, out3)) for pair in x_chunk(src, s, out)], sem)


def near_y_kernel(samples, grads, out1, out3, sem):
    run_copies([pair for s, out in ((1, out1), (3, out3)) for pair in y_chunk(samples, grads, s, out)], sem)


def rest_kernel(src, samples, grads, running, far_x, far_y, own_x, own_y, previous, sem):
    zl, c, y = (lax.axis_index(name) for name in ("zl", "c", "y"))
    run_copies([
        *x_chunk(src, 2, far_x), *y_chunk(samples, grads, 2, far_y),
        *x_chunk(src, 0, own_x), *y_chunk(samples, grads, 0, own_y),
        (running.at[(zl * 2 + c) * 4 + y], previous),
    ], sem)


X_CHUNK = jax.ShapeDtypeStruct((4, 128, 2 * BG), jnp.bfloat16)
Y_CHUNK = jax.ShapeDtypeStruct((128, 4 * BA + 4 * BG), jnp.bfloat16)
PREVIOUS = jax.ShapeDtypeStruct((BA, BA), jnp.float32)


def pack(kernel, count, out_shape, *args):
    return pl.pallas_call(
        kernel,
        out_shape=out_shape,
        in_specs=[pl.BlockSpec(memory_space=pl.ANY)] * len(args),
        out_specs=[VMEM] * len(out_shape),
        scratch_shapes=[pltpu.SemaphoreType.DMA((count,))],
    )(*args)


def gram(v):
    return lax.dot_general(v, v, (((0,), (0,)), ((), ())), preferred_element_type=jnp.float32)


def grid_of(n):
    return (lax.broadcasted_iota(jnp.int32, (n, n), 0), lax.broadcasted_iota(jnp.int32, (n, n), 1))


def fold_block(cov, tiles, n):
    r, k = grid_of(128)
    corner = cov[128:256, 128:256]
    fold = jnp.where(r >= k, cov[0:128, 0:128], corner)
    diag = jnp.sum(jnp.where(r == k, corner, 0.0), axis=0, keepdims=True)
    tiles[n, 0:16] = fold.reshape(16, 8, 128)
    tiles[n, 16:32] = cov[128:256, 0:128].reshape(16, 8, 128)
    tiles[n, 32:40] = cov[256:BG, 0:128].reshape(8, 8, 128)
    tiles[n, 40:48] = cov[256:BG, 128:256].reshape(8, 8, 128)
    beside = jnp.concatenate([
        jnp.broadcast_to(diag[:, 0:64], (8, 64)),
        jnp.broadcast_to(diag[:, 64:128], (8, 64)),
        jnp.zeros((48, 64), jnp.float32),
    ], axis=0)
    tiles[n, 48:56] = jnp.concatenate([cov[256:BG, 256:BG], beside], axis=1).reshape(8, 8, 128)


def g_cov_kernel(i0, i1, i2, i3, own, other, rows, tiles):
    c = lax.axis_index("c")
    for s, ref in enumerate((i0, i1, i2, i3)):
        rows[s * 128:(s + 1) * 128, :] = ref[0]
    fold_block(gram(rows[:, 0:BGP]), tiles, 0)
    fold_block(gram(rows[:, 2 * BG - BGP:2 * BG])[BGP - BG:, BGP - BG:], tiles, 1)
    own[0] = tiles[c]
    other[0] = tiles[1 - c]


def g_cov(chunks):
    spec = pl.BlockSpec((1, 128, 2 * BG), lambda q: (q, 0, 0))
    out = pl.BlockSpec((1, 56, 8, 128), lambda q: (q, 0, 0, 0))
    return pl.pallas_call(
        g_cov_kernel,
        grid=(4,),
        out_shape=[jax.ShapeDtypeStruct((4, 56, 8, 128), jnp.float32)] * 2,
        in_specs=[spec] * 4,
        out_specs=[out] * 2,
        scratch_shapes=[pltpu.VMEM((512, 2 * BG), jnp.bfloat16), pltpu.VMEM((2, G_TILES, 8, 128), jnp.float32)],
        compiler_params=pltpu.CompilerParams(vmem_limit_bytes=16 << 20),
    )(*chunks)


def a_cov_kernel(i0, i1, i2, i3, own, other, rows, tiles):
    c = lax.axis_index("c")
    r, k = grid_of(128)
    for zl in range(2):
        for core in range(2):
            q = zl * 2 + core
            for s, ref in enumerate((i0, i1, i2, i3)):
                rows[s * 128:(s + 1) * 128, :] = ref[:, q * BA:(q + 1) * BA]
            cov = gram(rows[...])
            corner = cov[128:, 128:]
            fold = jnp.where(r >= k, cov[:128, :128], corner)
            diag = jnp.sum(jnp.where(r == k, corner, 0.0), axis=0, keepdims=True)
            tiles[core, 0:16] = cov[128:, :128].reshape(16, 8, 128)
            tiles[core, 16:32] = fold.reshape(16, 8, 128)
            tiles[core, 32] = jnp.broadcast_to(diag, (8, 128))
            tiles[core, 33:] = jnp.zeros((A_TILES - 33, 8, 128), jnp.float32)
        own[zl] = tiles[c]
        other[zl] = tiles[1 - c]


def a_cov(chunks):
    return pl.pallas_call(
        a_cov_kernel,
        out_shape=[jax.ShapeDtypeStruct((2, A_TILES, 8, 128), jnp.float32)] * 2,
        in_specs=[VMEM] * 4,
        out_specs=[VMEM] * 2,
        scratch_shapes=[pltpu.VMEM((512, BA), jnp.bfloat16), pltpu.VMEM((2, A_TILES, 8, 128), jnp.float32)],
        compiler_params=pltpu.CompilerParams(vmem_limit_bytes=16 << 20),
    )(*chunks)


def tile_shape(*dims):
    return jax.ShapeDtypeStruct((*dims, 8, 128), jnp.float32)


def local(kernel, out_shape, *args):
    return pl.pallas_call(
        kernel,
        out_shape=out_shape,
        in_specs=[VMEM] * len(args),
        out_specs=jax.tree.map(lambda _: VMEM, out_shape),
        compiler_params=pltpu.CompilerParams(vmem_limit_bytes=16 << 20),
    )(*args)


def cores_kernel(g_own, g_got, a_own, a_got, *outs):
    x, y = lax.axis_index("x"), lax.axis_index("y")
    for s in range(4):
        place = pl.ds(lax.rem(y + s, 4) * 14, 14)
        outs[s][...] = g_own[:, place] + g_got[:, place]
        place = pl.ds(lax.rem(x + s, 4) * 9, 9)
        outs[4 + s][...] = a_own[:, place] + a_got[:, place]


def lines_kernel(g0, g1, g2, g3, a0, a1, a2, a3, keep, turn):
    zl = lax.axis_index("zl")
    for out, side in ((keep, zl), (turn, 1 - zl)):
        for q in range(4):
            place = pl.ds(side * 7, 7)
            out[q * 7:q * 7 + 7] = (g0[q, place] + g1[q, place]) + (g2[q, place] + g3[q, place])
        out[28:] = (a0[side] + a1[side]) + (a2[side] + a3[side])


def pairs_kernel(keep, got, *outs):
    zh = lax.axis_index("zh")
    a_sum = keep[28:] + got[28:]
    for s in range(4):
        place = pl.ds(lax.rem(zh + s, 4) * 7, 7)
        outs[s][0:7] = keep[place] + got[place]
        outs[s][7:] = a_sum


def pieces_kernel(p0, p1, p2, p3, g_piece, a_piece):
    g_piece[...] = (p0[0:7] + p1[0:7]) + (p2[0:7] + p3[0:7])
    a_piece[...] = (p0[7:] + p1[7:]) + (p2[7:] + p3[7:])


def join_kernel(own, got, out):
    zl = lax.axis_index("zl")
    out[pl.ds(zl * 7, 7)] = own[...]
    out[pl.ds((1 - zl) * 7, 7)] = got[...]


def split(value):
    high = value.astype(jnp.bfloat16)
    return high, (value - high.astype(jnp.float32)).astype(jnp.bfloat16)


def dot3(left, right):
    dot = functools.partial(jnp.dot, preferred_element_type=jnp.float32)
    return dot(left[0], right[0]) + (dot(left[0], right[1]) + dot(left[1], right[0]))


def three(value):
    high, low = split(value)
    return high, high, low


def newton_even(matrix, identity, lhs, rhs):
    n = identity.shape[0]

    def put(approx, product):
        high, low = split(2.0 * identity - product)
        rhs[0:n], rhs[n:2 * n], rhs[2 * n:3 * n] = high, low, high
        for i, part in enumerate(three(product)):
            lhs[0:n, i * n:(i + 1) * n] = part
        for i, part in enumerate(three(approx)):
            lhs[n:2 * n, i * n:(i + 1) * n] = part

    trace = jnp.sum(matrix * identity)
    put(identity / trace, matrix / trace)

    def step(_, carry):
        both = jnp.dot(lhs[...], rhs[...], preferred_element_type=jnp.float32)
        put(both[n:], both[:n])
        return carry

    lax.fori_loop(0, ITERS - 1, step, 0)
    return jnp.dot(lhs[n:2 * n], rhs[...], preferred_element_type=jnp.float32)


def a_side_kernel(p0, p1, p2, p3, running, g0, g1, g2, g3, left, tiles, lhs, rhs, *, token_total):
    x = lax.axis_index("x")
    for s, got in enumerate((p0, p1, p2, p3)):
        tiles[pl.ds(lax.rem(x + 4 - s, 4) * 9, 9)] = got[...]
    r, k = grid_of(128)
    low = tiles[0:16].reshape(128, 128)
    fold = tiles[16:32].reshape(128, 128)
    diag = tiles[32][0:1]
    turned = fold.T
    top = jnp.where(r >= k, fold, turned)
    corner = jnp.where(r == k, jnp.broadcast_to(diag, (128, 128)), jnp.where(r < k, fold, turned))
    cov = jnp.concatenate([
        jnp.concatenate([top, low.T], axis=1), jnp.concatenate([low, corner], axis=1)
    ], axis=0)
    r, k = grid_of(BA)
    identity = jnp.where(r == k, 1.0, 0.0)
    mixed = factor_decay * running[...] + (1.0 - factor_decay) * cov / token_total
    inverse = newton_even(mixed + damping * identity, identity, lhs, rhs)
    summed = []
    for h in range(2):
        begin = 4 * BA + h * 2 * BG
        g = [ref[:, begin:begin + 2 * BG].astype(jnp.float32) for ref in (g0, g1, g2, g3)]
        summed.append((g[0] + g[1]) + (g[2] + g[3]))
    summed = jnp.concatenate(summed, axis=0)
    done = dot3(split(inverse), split(summed))
    for n in range(2):
        left[n] = done[:, n * BG:(n + 1) * BG]


def a_side(pieces, running, grads, token_total):
    return pl.pallas_call(
        functools.partial(a_side_kernel, token_total=token_total),
        out_shape=jax.ShapeDtypeStruct((2, BA, BG), jnp.float32),
        in_specs=[VMEM] * 9,
        out_specs=VMEM,
        scratch_shapes=[
            pltpu.VMEM((A_TILES, 8, 128), jnp.float32),
            pltpu.VMEM((2 * BA, 3 * BA), jnp.bfloat16), pltpu.VMEM((3 * BA, BA), jnp.bfloat16)
        ],
        compiler_params=pltpu.CompilerParams(vmem_limit_bytes=16 << 20),
        cost_estimate=pl.CostEstimate(flops=2_500_000_000, bytes_accessed=2_000_000, transcendentals=0),
    )(*pieces, running, *grads)


def turned_tail(main):
    tail = main[256:BG]
    return jnp.concatenate([tail, jnp.zeros_like(tail)], axis=0).T


HALF = jax.ShapeDtypeStruct((128, 2 * BG), jnp.bfloat16)


def unfold_block(tiles):
    r, k = grid_of(128)
    fold = tiles[0:16].reshape(128, 128)
    low = tiles[16:32].reshape(128, 128)
    last = tiles[48:56].reshape(64, 128)
    diag = jnp.concatenate([last[0:1, 64:128], last[8:9, 64:128]], axis=1)
    turned = fold.T
    first = jnp.where(r >= k, fold, turned)
    second = jnp.where(r == k, jnp.broadcast_to(diag, (128, 128)), jnp.where(r < k, fold, turned))
    bottom = [tiles[32:40].reshape(64, 128), tiles[40:48].reshape(64, 128)]
    main = jnp.concatenate([
        jnp.concatenate([first, low.T], axis=1),
        jnp.concatenate([low, second], axis=1),
        jnp.concatenate(bottom, axis=1),
    ], axis=0)
    empty = jnp.zeros((64, 128), jnp.float32)
    r, k = lax.broadcasted_iota(jnp.int32, (64, 128), 0), lax.broadcasted_iota(jnp.int32, (64, 128), 1)
    tail = jnp.concatenate([jnp.concatenate([part, empty], axis=0).T for part in bottom]
                           + [jnp.where(k < 64, last, 0.0)], axis=0)
    return main, tail


def g_put(lhs, rhs_main, rhs_tail, ident, product, approx):
    for rhs, same, value in ((rhs_main, ident[0], product[0]), (rhs_tail, ident[1], product[1])):
        high, low = split(2.0 * same - value)
        rhs[0:BG] = high
        rhs[BGP:BGP + BG] = low
        rhs[2 * BGP:2 * BGP + BG] = high
    for row, (main, tail) in ((0, product), (BG, approx)):
        for i, (part, edge) in enumerate(zip(three(main), three(tail))):
            lhs[row:row + BG, i * BGP:i * BGP + 256] = part
            lhs[row:row + BG, i * BGP + 256:(i + 1) * BGP] = edge


def half_rows(left, inverse):
    done = dot3(split(left), (inverse[0], inverse[1]))[:, 0:BG].astype(jnp.bfloat16)
    return jnp.concatenate([done[0:128], done[128:BA]], axis=1)


def g_side_kernel(p0, p1, p2, p3, running, left, out, rows, tiles, lhs, rhs_main, rhs_tail, *, token_total):
    c, y = lax.axis_index("c"), lax.axis_index("y")
    for s, got in enumerate((p0, p1, p2, p3)):
        tiles[pl.ds(lax.rem(y + 4 - s, 4) * 14, 14)] = got[...]
    new_sum = unfold_block(tiles)
    previous = running[c, :, 0:256], jnp.concatenate(
        [running[c, :, 256:BG], jnp.zeros((BG, 64), jnp.float32)], axis=1
    )
    r, k = lax.broadcasted_iota(jnp.int32, (BG, 256), 0), lax.broadcasted_iota(jnp.int32, (BG, 256), 1)
    ident = [jnp.where(r == k, 1.0, 0.0)]
    r, k = lax.broadcasted_iota(jnp.int32, (BG, 128), 0), lax.broadcasted_iota(jnp.int32, (BG, 128), 1)
    ident.append(jnp.where(r == k + 256, 1.0, 0.0))
    matrix = [
        (factor_decay * before + (1.0 - factor_decay) * cov / token_total) + damping * same
        for before, cov, same in zip(previous, new_sum, ident)
    ]
    trace = sum(jnp.sum(part * same) for part, same in zip(matrix, ident))
    rhs_main[...] = jnp.zeros(rhs_main.shape, jnp.bfloat16)
    rhs_tail[...] = jnp.zeros(rhs_tail.shape, jnp.bfloat16)
    put = functools.partial(g_put, lhs, rhs_main, rhs_tail, ident)
    put([part / trace for part in matrix], [same / trace for same in ident])

    def times(row):
        main = jnp.dot(lhs[row:row + BG], rhs_main[...], preferred_element_type=jnp.float32)
        corner = jnp.dot(lhs[row + 256:row + BG], rhs_tail[...], preferred_element_type=jnp.float32)
        return main, jnp.concatenate([turned_tail(main), corner], axis=0)

    def step(_, carry):
        product, approx = times(0), times(BG)
        put(product, approx)
        return carry

    lax.fori_loop(0, ITERS - 1, step, 0, unroll=True)
    main, tail = times(BG)
    out[0], out[1] = split(jnp.concatenate([main, tail], axis=1))
    rows[...] = half_rows(left[c], out)


def g_side(pieces, running, left, token_total):
    return pl.pallas_call(
        functools.partial(g_side_kernel, token_total=token_total),
        out_shape=[jax.ShapeDtypeStruct((2, BG, BGP), jnp.bfloat16), HALF],
        in_specs=[VMEM] * 6,
        out_specs=[VMEM] * 2,
        scratch_shapes=[
            pltpu.VMEM((G_TILES, 8, 128), jnp.float32),
            pltpu.VMEM((2 * BG, 3 * BGP), jnp.bfloat16),
            pltpu.VMEM((3 * BGP, 256), jnp.bfloat16),
            pltpu.VMEM((3 * BGP, 128), jnp.bfloat16),
        ],
        compiler_params=pltpu.CompilerParams(vmem_limit_bytes=16 << 20),
        cost_estimate=pl.CostEstimate(flops=6_000_000_000, bytes_accessed=3_000_000, transcendentals=0),
    )(*pieces, running, left)


def apply_kernel(left, theirs, rows):
    rows[...] = half_rows(left[1 - lax.axis_index("c")], theirs)


def assemble_kernel(*refs):
    first, second, out = refs[:4], refs[4:8], refs[8]
    c, y = lax.axis_index("c"), lax.axis_index("y")
    for s in range(4):
        mine, theirs = first[s][...], second[s][...]
        halves = jnp.where(c == 0, mine, theirs), jnp.where(c == 0, theirs, mine)
        start = pl.multiple_of(lax.rem(y + 4 - s, 4) * BA, BA)
        for h in range(2):
            out[pl.ds(start + h * 128, 128), :] = jnp.concatenate(
                [half[:, h * BG:(h + 1) * BG] for half in halves], axis=1
            )


def per_device(activations, out_grads, a_running, g_running, grad_partial):
    token_total = float(activations.shape[0] * 256)
    y = lax.axis_index("y")

    near_x = pack(near_x_kernel, 8, [X_CHUNK] * 2, out_grads)
    near_x, activations = lax.optimization_barrier((near_x, activations))
    near_y = pack(near_y_kernel, 12, [Y_CHUNK] * 2, activations, grad_partial)
    near_y, out_grads = lax.optimization_barrier((near_y, out_grads))
    far_x, far_y, own_x, own_y, a_previous = pack(
        rest_kernel, 21, [X_CHUNK, Y_CHUNK, X_CHUNK, Y_CHUNK, PREVIOUS],
        out_grads, activations, grad_partial, a_running,
    )
    g_in = [send(near_x[0], "x", 1), send(near_x[1], "x", 3)]
    y_in = [send(near_y[0], "y", 1), send(near_y[1], "y", 3)]
    g_in, far_x = lax.optimization_barrier((g_in, far_x))
    g_in, y_in, far_y = lax.optimization_barrier((g_in, y_in, far_y))
    g_in = [own_x, *g_in, send(far_x, "x", 2)]
    y_in = [own_y, *y_in, send(far_y, "y", 2)]

    a_own, a_other = a_cov(y_in)
    g_in, a_own, a_other = lax.optimization_barrier((g_in, a_own, a_other))
    g_own, g_other = g_cov(g_in)
    cut = local(
        cores_kernel, [tile_shape(4, 14)] * 4 + [tile_shape(2, 9)] * 4,
        g_own, swap_cores(g_other), a_own, swap_cores(a_other),
    )
    lines = lax.optimization_barrier(send_round("y", cut[:4]) + send_round("x", cut[4:]))
    keep, turn = local(lines_kernel, [tile_shape(37)] * 2, *lines)
    cut = local(pairs_kernel, [tile_shape(16)] * 4, keep, swap_pair(turn))
    g_piece, a_piece = local(pieces_kernel, [tile_shape(7), tile_shape(9)], *send_round("zh", cut))

    a_pieces = send_round("x", [a_piece] * 4)
    g_pair = local(join_kernel, tile_shape(14), g_piece, swap_pair(g_piece))
    g_pieces = send_round("y", [g_pair] * 4)
    left = a_side(a_pieces, a_previous, y_in, token_total)
    g_pieces, left = lax.optimization_barrier((g_pieces, left))
    inverse, first = g_side(g_pieces, g_running, left, token_total)
    second = local(apply_kernel, HALF, left, swap_cores(inverse))
    parts = send_round("y", [first] * 4) + send_round("y", [second] * 4)
    return local(assemble_kernel, jax.ShapeDtypeStruct((4 * BA, 2 * BG), jnp.bfloat16), *parts)


def solution(mesh):
    fine = Mesh(mesh.devices.reshape(4, 4, 2, 2, 4), ("zh", "x", "zl", "c", "y"))
    tokens = P(("zh", "x", "zl", "c", "y"), None)
    placed = (tokens, tokens, P(), P(("zh", "x"), None, None), P("y", ("zl", "c"), ("zh", "x")))
    return jax.shard_map(
        per_device,
        mesh=fine,
        in_specs=placed,
        out_specs=P(("zl", "c"), ("zh", "x")),
        check_vma=False,
    )
```

```python
import functools

import jax
import jax.numpy as jnp
from jax import lax
from jax.experimental import pallas as pl
from jax.experimental.pallas import tpu as pltpu
from jax.sharding import Mesh, PartitionSpec as P

BA = 256
BG = 320
BGP = 384
ITERS = 8
G_TILES = 56
A_TILES = 36

factor_decay = 0.9
damping = 0.1

VMEM = pl.BlockSpec(memory_space=pltpu.VMEM)


def swap_cores(value):
    return lax.ppermute(value, "c", [(0, 1), (1, 0)])


def send(value, axis, s):
    return lax.ppermute(value, axis, [(i, (i + s) % 4) for i in range(4)])


def swap_pair(value):
    return lax.ppermute(value, "zl", [(0, 1), (1, 0)])


def send_round(axis, chunks):
    return [chunks[0]] + [send(chunks[s], axis, s) for s in range(1, 4)]


def run_copies(pairs, sem):
    copies = [pltpu.make_async_copy(src, dst, sem.at[i]) for i, (src, dst) in enumerate(pairs)]
    for copy in copies:
        copy.start()
    for copy in copies:
        copy.wait()


def x_chunk(src, s, out):
    peer = lax.rem(lax.axis_index("x") + s, 4)
    for q in range(4):
        start = pl.multiple_of((q * 4 + peer) * 2 * BG, 128)
        yield src.at[:, pl.ds(start, 2 * BG)], out.at[q]


def y_chunk(samples, grads, s, out):
    peer = lax.rem(lax.axis_index("y") + s, 4)
    for q in range(4):
        start = pl.multiple_of((q * 4 + peer) * BA, 128)
        yield samples.at[:, pl.ds(start, BA)], out.at[:, pl.ds(q * BA, BA)]
    for h in range(2):
        start = pl.multiple_of(peer * BA + h * 128, 128)
        yield grads.at[0, pl.ds(start, 128), :], out.at[:, pl.ds(4 * BA + h * 2 * BG, 2 * BG)]


def near_x_kernel(src, out1, out3, sem):
    run_copies([pair for s, out in ((1, out1), (3, out3)) for pair in x_chunk(src, s, out)], sem)


def near_y_kernel(samples, grads, out1, out3, sem):
    run_copies([pair for s, out in ((1, out1), (3, out3)) for pair in y_chunk(samples, grads, s, out)], sem)


def rest_kernel(src, samples, grads, running, far_x, far_y, own_x, own_y, previous, sem):
    zl, c, y = (lax.axis_index(name) for name in ("zl", "c", "y"))
    run_copies([
        *x_chunk(src, 2, far_x), *y_chunk(samples, grads, 2, far_y),
        *x_chunk(src, 0, own_x), *y_chunk(samples, grads, 0, own_y),
        (running.at[(zl * 2 + c) * 4 + y], previous),
    ], sem)


X_CHUNK = jax.ShapeDtypeStruct((4, 128, 2 * BG), jnp.bfloat16)
Y_CHUNK = jax.ShapeDtypeStruct((128, 4 * BA + 4 * BG), jnp.bfloat16)
PREVIOUS = jax.ShapeDtypeStruct((BA, BA), jnp.float32)


def pack(kernel, count, out_shape, *args):
    return pl.pallas_call(
        kernel,
        out_shape=out_shape,
        in_specs=[pl.BlockSpec(memory_space=pl.ANY)] * len(args),
        out_specs=[VMEM] * len(out_shape),
        scratch_shapes=[pltpu.SemaphoreType.DMA((count,))],
    )(*args)


def gram(v):
    return lax.dot_general(v, v, (((0,), (0,)), ((), ())), preferred_element_type=jnp.float32)


def grid_of(n):
    return (lax.broadcasted_iota(jnp.int32, (n, n), 0), lax.broadcasted_iota(jnp.int32, (n, n), 1))


def fold_block(cov, tiles, n):
    r, k = grid_of(128)
    corner = cov[128:256, 128:256]
    fold = jnp.where(r >= k, cov[0:128, 0:128], corner)
    diag = jnp.sum(jnp.where(r == k, corner, 0.0), axis=0, keepdims=True)
    tiles[n, 0:16] = fold.reshape(16, 8, 128)
    tiles[n, 16:32] = cov[128:256, 0:128].reshape(16, 8, 128)
    tiles[n, 32:40] = cov[256:BG, 0:128].reshape(8, 8, 128)
    tiles[n, 40:48] = cov[256:BG, 128:256].reshape(8, 8, 128)
    beside = jnp.concatenate([
        jnp.broadcast_to(diag[:, 0:64], (8, 64)),
        jnp.broadcast_to(diag[:, 64:128], (8, 64)),
        jnp.zeros((48, 64), jnp.float32),
    ], axis=0)
    tiles[n, 48:56] = jnp.concatenate([cov[256:BG, 256:BG], beside], axis=1).reshape(8, 8, 128)


def g_cov_kernel(i0, own_before, other_before, own, other, rows, tiles):
    c = lax.axis_index("c")
    for q in range(4):
        rows[q] = i0[q]
        fold_block(gram(rows[q, :, 0:BGP]), tiles.at[q], 0)
        fold_block(gram(rows[q, :, 2 * BG - BGP:2 * BG])[BGP - BG:, BGP - BG:], tiles.at[q], 1)
        own[q] = tiles[q, c] + own_before[q]
        other[q] = tiles[q, 1 - c] + other_before[q]


def g_cov_first_kernel(i0, i1, i2, own, other, rows, tiles):
    c = lax.axis_index("c")
    for q in range(4):
        for s, ref in enumerate((i0, i1, i2)):
            rows[q, s * 128:(s + 1) * 128, :] = ref[q]
        fold_block(gram(rows[q, :, 0:BGP]), tiles.at[q], 0)
        fold_block(gram(rows[q, :, 2 * BG - BGP:2 * BG])[BGP - BG:, BGP - BG:], tiles.at[q], 1)
        own[q] = tiles[q, c]
        other[q] = tiles[q, 1 - c]


def a_cov_blocks(chunks, rows, tiles):
    r, k = grid_of(128)
    for zl in range(2):
        for core in range(2):
            q = zl * 2 + core
            for s, ref in enumerate(chunks):
                rows[s * 128:(s + 1) * 128, :] = ref[:, q * BA:(q + 1) * BA]
            cov = gram(rows[...])
            corner = cov[128:, 128:]
            fold = jnp.where(r >= k, cov[:128, :128], corner)
            diag = jnp.sum(jnp.where(r == k, corner, 0.0), axis=0, keepdims=True)
            tiles[core, 0:16] = cov[128:, :128].reshape(16, 8, 128)
            tiles[core, 16:32] = fold.reshape(16, 8, 128)
            tiles[core, 32] = jnp.broadcast_to(diag, (8, 128))
            tiles[core, 33:] = jnp.zeros((A_TILES - 33, 8, 128), jnp.float32)
        yield zl


def a_cov_first_kernel(i0, i1, i2, own, other, rows, tiles):
    c = lax.axis_index("c")
    for zl in a_cov_blocks((i0, i1, i2), rows, tiles):
        own[zl] = tiles[c]
        other[zl] = tiles[1 - c]


def a_cov_kernel(i0, own_before, other_before, own, other, rows, tiles):
    c = lax.axis_index("c")
    for zl in a_cov_blocks((i0,), rows, tiles):
        own[zl] = tiles[c] + own_before[zl]
        other[zl] = tiles[1 - c] + other_before[zl]


def cov(kernel, out_dims, rows, tiles, *args):
    return pl.pallas_call(
        kernel,
        out_shape=[jax.ShapeDtypeStruct((*out_dims, 8, 128), jnp.float32)] * 2,
        in_specs=[VMEM] * len(args),
        out_specs=[VMEM] * 2,
        scratch_shapes=[pltpu.VMEM(rows, jnp.bfloat16), pltpu.VMEM((*tiles, 8, 128), jnp.float32)],
        compiler_params=pltpu.CompilerParams(vmem_limit_bytes=16 << 20),
        cost_estimate=pl.CostEstimate(flops=1_500_000_000, bytes_accessed=4_000_000, transcendentals=0),
    )(*args)


def g_cov_first(chunks):
    return cov(g_cov_first_kernel, (4, 56), (4, 384, 2 * BG), (4, 2, G_TILES), *chunks)


def g_cov(chunk, before):
    return cov(g_cov_kernel, (4, 56), (4, 128, 2 * BG), (4, 2, G_TILES), chunk, *before)


def a_cov_first(chunks):
    return cov(a_cov_first_kernel, (2, A_TILES), (384, BA), (2, A_TILES), *chunks)


def a_cov(chunk, before):
    return cov(a_cov_kernel, (2, A_TILES), (128, BA), (2, A_TILES), chunk, *before)


def tile_shape(*dims):
    return jax.ShapeDtypeStruct((*dims, 8, 128), jnp.float32)


def local(kernel, out_shape, *args):
    return pl.pallas_call(
        kernel,
        out_shape=out_shape,
        in_specs=[VMEM] * len(args),
        out_specs=jax.tree.map(lambda _: VMEM, out_shape),
        compiler_params=pltpu.CompilerParams(vmem_limit_bytes=16 << 20),
    )(*args)


def cores_kernel(g_own, g_got, a_own, a_got, *outs):
    x, y = lax.axis_index("x"), lax.axis_index("y")
    for s in range(4):
        place = pl.ds(lax.rem(y + s, 4) * 14, 14)
        outs[s][...] = g_own[:, place] + g_got[:, place]
        place = pl.ds(lax.rem(x + s, 4) * 9, 9)
        outs[4 + s][...] = a_own[:, place] + a_got[:, place]


def lines_kernel(g0, g1, g2, g3, a0, a1, a2, a3, keep, turn):
    zl = lax.axis_index("zl")
    for out, side in ((keep, zl), (turn, 1 - zl)):
        for q in range(4):
            place = pl.ds(side * 7, 7)
            out[q * 7:q * 7 + 7] = (g0[q, place] + g1[q, place]) + (g2[q, place] + g3[q, place])
        out[28:] = (a0[side] + a1[side]) + (a2[side] + a3[side])


def pairs_kernel(keep, got, *outs):
    zh = lax.axis_index("zh")
    a_sum = keep[28:] + got[28:]
    for s in range(4):
        place = pl.ds(lax.rem(zh + s, 4) * 7, 7)
        outs[s][0:7] = keep[place] + got[place]
        outs[s][7:] = a_sum


def pieces_kernel(p0, p1, p2, p3, g_piece, a_piece):
    g_piece[...] = (p0[0:7] + p1[0:7]) + (p2[0:7] + p3[0:7])
    a_piece[...] = (p0[7:] + p1[7:]) + (p2[7:] + p3[7:])


def join_kernel(own, got, out):
    zl = lax.axis_index("zl")
    out[pl.ds(zl * 7, 7)] = own[...]
    out[pl.ds((1 - zl) * 7, 7)] = got[...]


def split(value):
    high = value.astype(jnp.bfloat16)
    return high, (value - high.astype(jnp.float32)).astype(jnp.bfloat16)


def dot3(left, right):
    dot = functools.partial(jnp.dot, preferred_element_type=jnp.float32)
    return dot(left[0], right[0]) + (dot(left[0], right[1]) + dot(left[1], right[0]))


def three(value):
    high, low = split(value)
    return high, high, low


def newton_even(matrix, identity, lhs, rhs):
    n = identity.shape[0]

    def put(approx, product):
        high, low = split(2.0 * identity - product)
        rhs[0:n], rhs[n:2 * n], rhs[2 * n:3 * n] = high, low, high
        for i, part in enumerate(three(product)):
            lhs[0:n, i * n:(i + 1) * n] = part
        for i, part in enumerate(three(approx)):
            lhs[n:2 * n, i * n:(i + 1) * n] = part

    trace = jnp.sum(matrix * identity)
    put(identity / trace, matrix / trace)

    def step(_, carry):
        both = jnp.dot(lhs[...], rhs[...], preferred_element_type=jnp.float32)
        put(both[n:], both[:n])
        return carry

    lax.fori_loop(0, ITERS - 1, step, 0)
    return jnp.dot(lhs[n:2 * n], rhs[...], preferred_element_type=jnp.float32)


def a_side_kernel(p0, p1, p2, p3, running, g0, g1, g2, g3, left, tiles, lhs, rhs, *, token_total):
    x = lax.axis_index("x")
    for s, got in enumerate((p0, p1, p2, p3)):
        tiles[pl.ds(lax.rem(x + 4 - s, 4) * 9, 9)] = got[...]
    r, k = grid_of(128)
    low = tiles[0:16].reshape(128, 128)
    fold = tiles[16:32].reshape(128, 128)
    diag = tiles[32][0:1]
    turned = fold.T
    top = jnp.where(r >= k, fold, turned)
    corner = jnp.where(r == k, jnp.broadcast_to(diag, (128, 128)), jnp.where(r < k, fold, turned))
    cov = jnp.concatenate([
        jnp.concatenate([top, low.T], axis=1), jnp.concatenate([low, corner], axis=1)
    ], axis=0)
    r, k = grid_of(BA)
    identity = jnp.where(r == k, 1.0, 0.0)
    mixed = factor_decay * running[...] + (1.0 - factor_decay) * cov / token_total
    inverse = newton_even(mixed + damping * identity, identity, lhs, rhs)
    summed = []
    for h in range(2):
        begin = 4 * BA + h * 2 * BG
        g = [ref[:, begin:begin + 2 * BG].astype(jnp.float32) for ref in (g0, g1, g2, g3)]
        summed.append((g[0] + g[1]) + (g[2] + g[3]))
    summed = jnp.concatenate(summed, axis=0)
    done = dot3(split(inverse), split(summed))
    for n in range(2):
        left[n] = done[:, n * BG:(n + 1) * BG]


def a_side(pieces, running, grads, token_total):
    return pl.pallas_call(
        functools.partial(a_side_kernel, token_total=token_total),
        out_shape=jax.ShapeDtypeStruct((2, BA, BG), jnp.float32),
        in_specs=[VMEM] * 9,
        out_specs=VMEM,
        scratch_shapes=[
            pltpu.VMEM((A_TILES, 8, 128), jnp.float32),
            pltpu.VMEM((2 * BA, 3 * BA), jnp.bfloat16), pltpu.VMEM((3 * BA, BA), jnp.bfloat16)
        ],
        compiler_params=pltpu.CompilerParams(vmem_limit_bytes=16 << 20),
        cost_estimate=pl.CostEstimate(flops=2_500_000_000, bytes_accessed=2_000_000, transcendentals=0),
    )(*pieces, running, *grads)


def turned_tail(main):
    tail = main[256:BG]
    return jnp.concatenate([tail, jnp.zeros_like(tail)], axis=0).T


HALF = jax.ShapeDtypeStruct((128, 2 * BG), jnp.bfloat16)


def unfold_block(tiles):
    r, k = grid_of(128)
    fold = tiles[0:16].reshape(128, 128)
    low = tiles[16:32].reshape(128, 128)
    last = tiles[48:56].reshape(64, 128)
    diag = jnp.concatenate([last[0:1, 64:128], last[8:9, 64:128]], axis=1)
    turned = fold.T
    first = jnp.where(r >= k, fold, turned)
    second = jnp.where(r == k, jnp.broadcast_to(diag, (128, 128)), jnp.where(r < k, fold, turned))
    bottom = [tiles[32:40].reshape(64, 128), tiles[40:48].reshape(64, 128)]
    main = jnp.concatenate([
        jnp.concatenate([first, low.T], axis=1),
        jnp.concatenate([low, second], axis=1),
        jnp.concatenate(bottom, axis=1),
    ], axis=0)
    empty = jnp.zeros((64, 128), jnp.float32)
    r, k = lax.broadcasted_iota(jnp.int32, (64, 128), 0), lax.broadcasted_iota(jnp.int32, (64, 128), 1)
    tail = jnp.concatenate([jnp.concatenate([part, empty], axis=0).T for part in bottom]
                           + [jnp.where(k < 64, last, 0.0)], axis=0)
    return main, tail


def g_put(lhs, rhs_main, rhs_tail, ident, product, approx):
    for rhs, same, value in ((rhs_main, ident[0], product[0]), (rhs_tail, ident[1], product[1])):
        high, low = split(2.0 * same - value)
        rhs[0:BG] = high
        rhs[BGP:BGP + BG] = low
        rhs[2 * BGP:2 * BGP + BG] = high
    for row, (main, tail) in ((0, product), (BG, approx)):
        for i, (part, edge) in enumerate(zip(three(main), three(tail))):
            lhs[row:row + BG, i * BGP:i * BGP + 256] = part
            lhs[row:row + BG, i * BGP + 256:(i + 1) * BGP] = edge


def half_rows(left, inverse):
    done = dot3(split(left), (inverse[0], inverse[1]))[:, 0:BG].astype(jnp.bfloat16)
    return jnp.concatenate([done[0:128], done[128:BA]], axis=1)


def g_side_kernel(p0, p1, p2, p3, running, left, out, rows, tiles, lhs, rhs_main, rhs_tail, *, token_total):
    c, y = lax.axis_index("c"), lax.axis_index("y")
    for s, got in enumerate((p0, p1, p2, p3)):
        tiles[pl.ds(lax.rem(y + 4 - s, 4) * 14, 14)] = got[...]
    new_sum = unfold_block(tiles)
    previous = running[c, :, 0:256], jnp.concatenate(
        [running[c, :, 256:BG], jnp.zeros((BG, 64), jnp.float32)], axis=1
    )
    r, k = lax.broadcasted_iota(jnp.int32, (BG, 256), 0), lax.broadcasted_iota(jnp.int32, (BG, 256), 1)
    ident = [jnp.where(r == k, 1.0, 0.0)]
    r, k = lax.broadcasted_iota(jnp.int32, (BG, 128), 0), lax.broadcasted_iota(jnp.int32, (BG, 128), 1)
    ident.append(jnp.where(r == k + 256, 1.0, 0.0))
    matrix = [
        (factor_decay * before + (1.0 - factor_decay) * cov / token_total) + damping * same
        for before, cov, same in zip(previous, new_sum, ident)
    ]
    trace = sum(jnp.sum(part * same) for part, same in zip(matrix, ident))
    rhs_main[...] = jnp.zeros(rhs_main.shape, jnp.bfloat16)
    rhs_tail[...] = jnp.zeros(rhs_tail.shape, jnp.bfloat16)
    put = functools.partial(g_put, lhs, rhs_main, rhs_tail, ident)
    put([part / trace for part in matrix], [same / trace for same in ident])

    def times(row):
        main = jnp.dot(lhs[row:row + BG], rhs_main[...], preferred_element_type=jnp.float32)
        corner = jnp.dot(lhs[row + 256:row + BG], rhs_tail[...], preferred_element_type=jnp.float32)
        return main, jnp.concatenate([turned_tail(main), corner], axis=0)

    def step(_, carry):
        product, approx = times(0), times(BG)
        put(product, approx)
        return carry

    lax.fori_loop(0, ITERS - 1, step, 0, unroll=True)
    main, tail = times(BG)
    out[0], out[1] = split(jnp.concatenate([main, tail], axis=1))
    rows[...] = half_rows(left[c], out)


def g_side(pieces, running, left, token_total):
    return pl.pallas_call(
        functools.partial(g_side_kernel, token_total=token_total),
        out_shape=[jax.ShapeDtypeStruct((2, BG, BGP), jnp.bfloat16), HALF],
        in_specs=[VMEM] * 6,
        out_specs=[VMEM] * 2,
        scratch_shapes=[
            pltpu.VMEM((G_TILES, 8, 128), jnp.float32),
            pltpu.VMEM((2 * BG, 3 * BGP), jnp.bfloat16),
            pltpu.VMEM((3 * BGP, 256), jnp.bfloat16),
            pltpu.VMEM((3 * BGP, 128), jnp.bfloat16),
        ],
        compiler_params=pltpu.CompilerParams(vmem_limit_bytes=16 << 20),
        cost_estimate=pl.CostEstimate(flops=6_000_000_000, bytes_accessed=3_000_000, transcendentals=0),
    )(*pieces, running, left)


def apply_kernel(left, theirs, rows):
    rows[...] = half_rows(left[1 - lax.axis_index("c")], theirs)


def assemble_kernel(*refs):
    first, second, out = refs[:4], refs[4:8], refs[8]
    c, y = lax.axis_index("c"), lax.axis_index("y")
    for s in range(4):
        mine, theirs = first[s][...], second[s][...]
        halves = jnp.where(c == 0, mine, theirs), jnp.where(c == 0, theirs, mine)
        start = pl.multiple_of(lax.rem(y + 4 - s, 4) * BA, BA)
        for h in range(2):
            out[pl.ds(start + h * 128, 128), :] = jnp.concatenate(
                [half[:, h * BG:(h + 1) * BG] for half in halves], axis=1
            )


def per_device(activations, out_grads, a_running, g_running, grad_partial):
    token_total = float(activations.shape[0] * 256)
    y = lax.axis_index("y")

    near_x = pack(near_x_kernel, 8, [X_CHUNK] * 2, out_grads)
    near_x, activations = lax.optimization_barrier((near_x, activations))
    near_y = pack(near_y_kernel, 12, [Y_CHUNK] * 2, activations, grad_partial)
    near_y, out_grads = lax.optimization_barrier((near_y, out_grads))
    far_x, far_y, own_x, own_y, a_previous = pack(
        rest_kernel, 21, [X_CHUNK, Y_CHUNK, X_CHUNK, Y_CHUNK, PREVIOUS],
        out_grads, activations, grad_partial, a_running,
    )
    g_in = [send(near_x[0], "x", 1), send(near_x[1], "x", 3)]
    y_in = [send(near_y[0], "y", 1), send(near_y[1], "y", 3)]
    g_in, far_x = lax.optimization_barrier((g_in, far_x))
    g_in, y_in, far_y = lax.optimization_barrier((g_in, y_in, far_y))
    far_x, far_y = send(far_x, "x", 2), send(far_y, "y", 2)

    g_before = g_cov_first([own_x, *g_in])
    a_before = a_cov_first([own_y, *y_in])
    a_own, a_other = a_cov(far_y, a_before)
    far_x, a_own, a_other = lax.optimization_barrier((far_x, a_own, a_other))
    g_own, g_other = g_cov(far_x, g_before)
    cut = local(
        cores_kernel, [tile_shape(4, 14)] * 4 + [tile_shape(2, 9)] * 4,
        g_own, swap_cores(g_other), a_own, swap_cores(a_other),
    )
    lines = lax.optimization_barrier(send_round("y", cut[:4]) + send_round("x", cut[4:]))
    keep, turn = local(lines_kernel, [tile_shape(37)] * 2, *lines)
    cut = local(pairs_kernel, [tile_shape(16)] * 4, keep, swap_pair(turn))
    g_piece, a_piece = local(pieces_kernel, [tile_shape(7), tile_shape(9)], *send_round("zh", cut))

    a_pieces = send_round("x", [a_piece] * 4)
    g_pair = local(join_kernel, tile_shape(14), g_piece, swap_pair(g_piece))
    g_pieces = send_round("y", [g_pair] * 4)
    left = a_side(a_pieces, a_previous, [own_y, *y_in, far_y], token_total)
    g_pieces, left = lax.optimization_barrier((g_pieces, left))
    inverse, first = g_side(g_pieces, g_running, left, token_total)
    second = local(apply_kernel, HALF, left, swap_cores(inverse))
    parts = send_round("y", [first] * 4) + send_round("y", [second] * 4)
    return local(assemble_kernel, jax.ShapeDtypeStruct((4 * BA, 2 * BG), jnp.bfloat16), *parts)


def solution(mesh):
    fine = Mesh(mesh.devices.reshape(4, 4, 2, 2, 4), ("zh", "x", "zl", "c", "y"))
    tokens = P(("zh", "x", "zl", "c", "y"), None)
    placed = (tokens, tokens, P(), P(("zh", "x"), None, None), P("y", ("zl", "c"), ("zh", "x")))
    return jax.shard_map(
        per_device,
        mesh=fine,
        in_specs=placed,
        out_specs=P(("zl", "c"), ("zh", "x")),
        check_vma=False,
    )
```

```python
import functools

import jax
import jax.numpy as jnp
from jax import lax
from jax.experimental import pallas as pl
from jax.experimental.pallas import tpu as pltpu
from jax.sharding import Mesh, PartitionSpec as P

BA = 256
BG = 320
BGP = 384
ITERS = 8
G_TILES = 56
A_TILES = 36

factor_decay = 0.9
damping = 0.1

VMEM = pl.BlockSpec(memory_space=pltpu.VMEM)


def swap_cores(value):
    return lax.ppermute(value, "c", [(0, 1), (1, 0)])


def send(value, axis, s):
    return lax.ppermute(value, axis, [(i, (i + s) % 4) for i in range(4)])


def swap_pair(value):
    return lax.ppermute(value, "zl", [(0, 1), (1, 0)])


def send_round(axis, chunks):
    return [chunks[0]] + [send(chunks[s], axis, s) for s in range(1, 4)]


def run_copies(pairs, sem):
    copies = [pltpu.make_async_copy(src, dst, sem.at[i]) for i, (src, dst) in enumerate(pairs)]
    for copy in copies:
        copy.start()
    for copy in copies:
        copy.wait()


def x_chunk(src, s, out):
    peer = lax.rem(lax.axis_index("x") + s, 4)
    for q in range(4):
        start = pl.multiple_of((q * 4 + peer) * 2 * BG, 128)
        yield src.at[:, pl.ds(start, 2 * BG)], out.at[q]


def y_chunk(samples, grads, s, out):
    peer = lax.rem(lax.axis_index("y") + s, 4)
    for q in range(4):
        start = pl.multiple_of((q * 4 + peer) * BA, 128)
        yield samples.at[:, pl.ds(start, BA)], out.at[:, pl.ds(q * BA, BA)]
    for h in range(2):
        start = pl.multiple_of(peer * BA + h * 128, 128)
        yield grads.at[0, pl.ds(start, 128), :], out.at[:, pl.ds(4 * BA + h * 2 * BG, 2 * BG)]


def near_x_kernel(src, out1, out3, sem):
    run_copies([pair for s, out in ((1, out1), (3, out3)) for pair in x_chunk(src, s, out)], sem)


def near_y_kernel(samples, grads, out1, out3, sem):
    run_copies([pair for s, out in ((1, out1), (3, out3)) for pair in y_chunk(samples, grads, s, out)], sem)


def rest_kernel(src, samples, grads, running, far_x, far_y, own_x, own_y, previous, sem):
    zl, c, y = (lax.axis_index(name) for name in ("zl", "c", "y"))
    run_copies([
        *x_chunk(src, 2, far_x), *y_chunk(samples, grads, 2, far_y),
        *x_chunk(src, 0, own_x), *y_chunk(samples, grads, 0, own_y),
        (running.at[(zl * 2 + c) * 4 + y], previous),
    ], sem)


X_CHUNK = jax.ShapeDtypeStruct((4, 128, 2 * BG), jnp.bfloat16)
Y_CHUNK = jax.ShapeDtypeStruct((128, 4 * BA + 4 * BG), jnp.bfloat16)
PREVIOUS = jax.ShapeDtypeStruct((BA, BA), jnp.float32)


def pack(kernel, count, out_shape, *args):
    return pl.pallas_call(
        kernel,
        out_shape=out_shape,
        in_specs=[pl.BlockSpec(memory_space=pl.ANY)] * len(args),
        out_specs=[VMEM] * len(out_shape),
        scratch_shapes=[pltpu.SemaphoreType.DMA((count,))],
    )(*args)


def gram(v):
    return lax.dot_general(v, v, (((0,), (0,)), ((), ())), preferred_element_type=jnp.float32)


def grid_of(n):
    return (lax.broadcasted_iota(jnp.int32, (n, n), 0), lax.broadcasted_iota(jnp.int32, (n, n), 1))


def fold_block(cov, tiles, n):
    r, k = grid_of(128)
    corner = cov[128:256, 128:256]
    fold = jnp.where(r >= k, cov[0:128, 0:128], corner)
    diag = jnp.sum(jnp.where(r == k, corner, 0.0), axis=0, keepdims=True)
    tiles[n, 0:16] = fold.reshape(16, 8, 128)
    tiles[n, 16:32] = cov[128:256, 0:128].reshape(16, 8, 128)
    tiles[n, 32:40] = cov[256:BG, 0:128].reshape(8, 8, 128)
    tiles[n, 40:48] = cov[256:BG, 128:256].reshape(8, 8, 128)
    beside = jnp.concatenate([
        jnp.broadcast_to(diag[:, 0:64], (8, 64)),
        jnp.broadcast_to(diag[:, 64:128], (8, 64)),
        jnp.zeros((48, 64), jnp.float32),
    ], axis=0)
    tiles[n, 48:56] = jnp.concatenate([cov[256:BG, 256:BG], beside], axis=1).reshape(8, 8, 128)


def g_cov_kernel(i0, own_before, other_before, own, other, rows, tiles):
    c = lax.axis_index("c")
    for q in range(4):
        rows[q] = i0[q]
        fold_block(gram(rows[q, :, 0:BGP]), tiles.at[q], 0)
        fold_block(gram(rows[q, :, 2 * BG - BGP:2 * BG])[BGP - BG:, BGP - BG:], tiles.at[q], 1)
        own[q] = tiles[q, c] + own_before[q]
        other[q] = tiles[q, 1 - c] + other_before[q]


def g_cov_first_kernel(i0, i1, i2, own, other, rows, tiles):
    c = lax.axis_index("c")
    for q in range(4):
        for s, ref in enumerate((i0, i1, i2)):
            rows[q, s * 128:(s + 1) * 128, :] = ref[q]
        fold_block(gram(rows[q, :, 0:BGP]), tiles.at[q], 0)
        fold_block(gram(rows[q, :, 2 * BG - BGP:2 * BG])[BGP - BG:, BGP - BG:], tiles.at[q], 1)
        own[q] = tiles[q, c]
        other[q] = tiles[q, 1 - c]


def a_cov_blocks(chunks, rows, tiles):
    r, k = grid_of(128)
    for zl in range(2):
        for core in range(2):
            q = zl * 2 + core
            for s, ref in enumerate(chunks):
                rows[s * 128:(s + 1) * 128, :] = ref[:, q * BA:(q + 1) * BA]
            cov = gram(rows[...])
            corner = cov[128:, 128:]
            fold = jnp.where(r >= k, cov[:128, :128], corner)
            diag = jnp.sum(jnp.where(r == k, corner, 0.0), axis=0, keepdims=True)
            tiles[core, 0:16] = cov[128:, :128].reshape(16, 8, 128)
            tiles[core, 16:32] = fold.reshape(16, 8, 128)
            tiles[core, 32] = jnp.broadcast_to(diag, (8, 128))
            tiles[core, 33:] = jnp.zeros((A_TILES - 33, 8, 128), jnp.float32)
        yield zl


def a_cov_first_kernel(i0, i1, i2, own, other, rows, tiles):
    c = lax.axis_index("c")
    for zl in a_cov_blocks((i0, i1, i2), rows, tiles):
        own[zl] = tiles[c]
        other[zl] = tiles[1 - c]


def a_cov_kernel(i0, own_before, other_before, own, other, rows, tiles):
    c = lax.axis_index("c")
    for zl in a_cov_blocks((i0,), rows, tiles):
        own[zl] = tiles[c] + own_before[zl]
        other[zl] = tiles[1 - c] + other_before[zl]


def cov(kernel, out_dims, rows, tiles, *args):
    return pl.pallas_call(
        kernel,
        out_shape=[jax.ShapeDtypeStruct((*out_dims, 8, 128), jnp.float32)] * 2,
        in_specs=[VMEM] * len(args),
        out_specs=[VMEM] * 2,
        scratch_shapes=[pltpu.VMEM(rows, jnp.bfloat16), pltpu.VMEM((*tiles, 8, 128), jnp.float32)],
        compiler_params=pltpu.CompilerParams(vmem_limit_bytes=16 << 20),
        cost_estimate=pl.CostEstimate(flops=1_500_000_000, bytes_accessed=4_000_000, transcendentals=0),
    )(*args)


def g_cov_first(chunks):
    return cov(g_cov_first_kernel, (4, 56), (4, 384, 2 * BG), (4, 2, G_TILES), *chunks)


def g_cov(chunk, before):
    return cov(g_cov_kernel, (4, 56), (4, 128, 2 * BG), (4, 2, G_TILES), chunk, *before)


def a_cov_first(chunks):
    return cov(a_cov_first_kernel, (2, A_TILES), (384, BA), (2, A_TILES), *chunks)


def a_cov(chunk, before):
    return cov(a_cov_kernel, (2, A_TILES), (128, BA), (2, A_TILES), chunk, *before)


def tile_shape(*dims):
    return jax.ShapeDtypeStruct((*dims, 8, 128), jnp.float32)


def local(kernel, out_shape, *args):
    return pl.pallas_call(
        kernel,
        out_shape=out_shape,
        in_specs=[VMEM] * len(args),
        out_specs=jax.tree.map(lambda _: VMEM, out_shape),
        compiler_params=pltpu.CompilerParams(vmem_limit_bytes=16 << 20),
    )(*args)


def cores_kernel(g_own, g_got, a_own, a_got, *outs):
    x, y = lax.axis_index("x"), lax.axis_index("y")
    for s in range(4):
        place = pl.ds(lax.rem(y + s, 4) * 14, 14)
        outs[s][...] = g_own[:, place] + g_got[:, place]
        place = pl.ds(lax.rem(x + s, 4) * 9, 9)
        outs[4 + s][...] = a_own[:, place] + a_got[:, place]


def lines_kernel(g0, g1, g2, g3, a0, a1, a2, a3, keep, turn):
    zl = lax.axis_index("zl")
    for out, side in ((keep, zl), (turn, 1 - zl)):
        for q in range(4):
            place = pl.ds(side * 7, 7)
            out[q * 7:q * 7 + 7] = (g0[q, place] + g1[q, place]) + (g2[q, place] + g3[q, place])
        out[28:] = (a0[side] + a1[side]) + (a2[side] + a3[side])


def pairs_kernel(keep, got, *outs):
    zh = lax.axis_index("zh")
    a_sum = keep[28:] + got[28:]
    for s in range(4):
        place = pl.ds(lax.rem(zh + s, 4) * 7, 7)
        outs[s][0:7] = keep[place] + got[place]
        outs[s][7:] = a_sum


def pieces_kernel(p0, p1, p2, p3, g_piece, a_piece):
    g_piece[...] = (p0[0:7] + p1[0:7]) + (p2[0:7] + p3[0:7])
    a_piece[...] = (p0[7:] + p1[7:]) + (p2[7:] + p3[7:])


def join_kernel(own, got, out):
    zl = lax.axis_index("zl")
    out[pl.ds(zl * 7, 7)] = own[...]
    out[pl.ds((1 - zl) * 7, 7)] = got[...]


def split(value):
    high = value.astype(jnp.bfloat16)
    return high, (value - high.astype(jnp.float32)).astype(jnp.bfloat16)


def dot3(left, right):
    dot = functools.partial(jnp.dot, preferred_element_type=jnp.float32)
    return dot(left[0], right[0]) + (dot(left[0], right[1]) + dot(left[1], right[0]))


def three(value):
    high, low = split(value)
    return high, high, low


def newton_even(matrix, identity, lhs, rhs):
    n = identity.shape[0]

    def put(approx, product):
        high, low = split(2.0 * identity - product)
        rhs[0:n], rhs[n:2 * n], rhs[2 * n:3 * n] = high, low, high
        for i, part in enumerate(three(product)):
            lhs[0:n, i * n:(i + 1) * n] = part
        for i, part in enumerate(three(approx)):
            lhs[n:2 * n, i * n:(i + 1) * n] = part

    trace = jnp.sum(matrix * identity)
    scaled = matrix / trace
    approx = (2.0 * identity - scaled) / trace
    put(approx, scaled)
    put(approx, jnp.dot(lhs[0:n], rhs[...], preferred_element_type=jnp.float32))

    def step(_, carry):
        both = jnp.dot(lhs[...], rhs[...], preferred_element_type=jnp.float32)
        put(both[n:], both[:n])
        return carry

    lax.fori_loop(0, ITERS - 2, step, 0)
    return jnp.dot(lhs[n:2 * n], rhs[...], preferred_element_type=jnp.float32)


def a_side_kernel(p0, p1, p2, p3, running, g0, g1, g2, g3, left, tiles, lhs, rhs, *, token_total):
    x = lax.axis_index("x")
    for s, got in enumerate((p0, p1, p2, p3)):
        tiles[pl.ds(lax.rem(x + 4 - s, 4) * 9, 9)] = got[...]
    r, k = grid_of(128)
    low = tiles[0:16].reshape(128, 128)
    fold = tiles[16:32].reshape(128, 128)
    diag = tiles[32][0:1]
    turned = fold.T
    top = jnp.where(r >= k, fold, turned)
    corner = jnp.where(r == k, jnp.broadcast_to(diag, (128, 128)), jnp.where(r < k, fold, turned))
    cov = jnp.concatenate([
        jnp.concatenate([top, low.T], axis=1), jnp.concatenate([low, corner], axis=1)
    ], axis=0)
    r, k = grid_of(BA)
    identity = jnp.where(r == k, 1.0, 0.0)
    mixed = factor_decay * running[...] + (1.0 - factor_decay) * cov / token_total
    inverse = newton_even(mixed + damping * identity, identity, lhs, rhs)
    summed = []
    for h in range(2):
        begin = 4 * BA + h * 2 * BG
        g = [ref[:, begin:begin + 2 * BG].astype(jnp.float32) for ref in (g0, g1, g2, g3)]
        summed.append((g[0] + g[1]) + (g[2] + g[3]))
    summed = jnp.concatenate(summed, axis=0)
    done = dot3(split(inverse), split(summed))
    for n in range(2):
        left[n] = done[:, n * BG:(n + 1) * BG]


def a_side(pieces, running, grads, token_total):
    return pl.pallas_call(
        functools.partial(a_side_kernel, token_total=token_total),
        out_shape=jax.ShapeDtypeStruct((2, BA, BG), jnp.float32),
        in_specs=[VMEM] * 9,
        out_specs=VMEM,
        scratch_shapes=[
            pltpu.VMEM((A_TILES, 8, 128), jnp.float32),
            pltpu.VMEM((2 * BA, 3 * BA), jnp.bfloat16), pltpu.VMEM((3 * BA, BA), jnp.bfloat16)
        ],
        compiler_params=pltpu.CompilerParams(vmem_limit_bytes=16 << 20),
        cost_estimate=pl.CostEstimate(flops=2_500_000_000, bytes_accessed=2_000_000, transcendentals=0),
    )(*pieces, running, *grads)


def turned_tail(main):
    tail = main[256:BG]
    return jnp.concatenate([tail, jnp.zeros_like(tail)], axis=0).T


HALF = jax.ShapeDtypeStruct((128, 2 * BG), jnp.bfloat16)


def unfold_block(tiles):
    r, k = grid_of(128)
    fold = tiles[0:16].reshape(128, 128)
    low = tiles[16:32].reshape(128, 128)
    last = tiles[48:56].reshape(64, 128)
    diag = jnp.concatenate([last[0:1, 64:128], last[8:9, 64:128]], axis=1)
    turned = fold.T
    first = jnp.where(r >= k, fold, turned)
    second = jnp.where(r == k, jnp.broadcast_to(diag, (128, 128)), jnp.where(r < k, fold, turned))
    bottom = [tiles[32:40].reshape(64, 128), tiles[40:48].reshape(64, 128)]
    main = jnp.concatenate([
        jnp.concatenate([first, low.T], axis=1),
        jnp.concatenate([low, second], axis=1),
        jnp.concatenate(bottom, axis=1),
    ], axis=0)
    empty = jnp.zeros((64, 128), jnp.float32)
    r, k = lax.broadcasted_iota(jnp.int32, (64, 128), 0), lax.broadcasted_iota(jnp.int32, (64, 128), 1)
    tail = jnp.concatenate([jnp.concatenate([part, empty], axis=0).T for part in bottom]
                           + [jnp.where(k < 64, last, 0.0)], axis=0)
    return main, tail


def g_put(lhs, rhs_main, rhs_tail, ident, product, approx):
    for rhs, same, value in ((rhs_main, ident[0], product[0]), (rhs_tail, ident[1], product[1])):
        high, low = split(2.0 * same - value)
        rhs[0:BG] = high
        rhs[BGP:BGP + BG] = low
        rhs[2 * BGP:2 * BGP + BG] = high
    for row, (main, tail) in ((0, product), (BG, approx)):
        for i, (part, edge) in enumerate(zip(three(main), three(tail))):
            lhs[row:row + BG, i * BGP:i * BGP + 256] = part
            lhs[row:row + BG, i * BGP + 256:(i + 1) * BGP] = edge


def half_rows(left, inverse):
    done = dot3(split(left), (inverse[0], inverse[1]))[:, 0:BG].astype(jnp.bfloat16)
    return jnp.concatenate([done[0:128], done[128:BA]], axis=1)


def g_side_kernel(p0, p1, p2, p3, running, left, out, rows, tiles, lhs, rhs_main, rhs_tail, *, token_total):
    c, y = lax.axis_index("c"), lax.axis_index("y")
    for s, got in enumerate((p0, p1, p2, p3)):
        tiles[pl.ds(lax.rem(y + 4 - s, 4) * 14, 14)] = got[...]
    new_sum = unfold_block(tiles)
    previous = running[c, :, 0:256], jnp.concatenate(
        [running[c, :, 256:BG], jnp.zeros((BG, 64), jnp.float32)], axis=1
    )
    r, k = lax.broadcasted_iota(jnp.int32, (BG, 256), 0), lax.broadcasted_iota(jnp.int32, (BG, 256), 1)
    ident = [jnp.where(r == k, 1.0, 0.0)]
    r, k = lax.broadcasted_iota(jnp.int32, (BG, 128), 0), lax.broadcasted_iota(jnp.int32, (BG, 128), 1)
    ident.append(jnp.where(r == k + 256, 1.0, 0.0))
    matrix = [
        (factor_decay * before + (1.0 - factor_decay) * cov / token_total) + damping * same
        for before, cov, same in zip(previous, new_sum, ident)
    ]
    trace = sum(jnp.sum(part * same) for part, same in zip(matrix, ident))
    rhs_main[...] = jnp.zeros(rhs_main.shape, jnp.bfloat16)
    rhs_tail[...] = jnp.zeros(rhs_tail.shape, jnp.bfloat16)
    put = functools.partial(g_put, lhs, rhs_main, rhs_tail, ident)
    scaled = [part / trace for part in matrix]
    approx = [(2.0 * same - part) / trace for same, part in zip(ident, scaled)]
    put(scaled, approx)

    def times(row):
        main = jnp.dot(lhs[row:row + BG], rhs_main[...], preferred_element_type=jnp.float32)
        corner = jnp.dot(lhs[row + 256:row + BG], rhs_tail[...], preferred_element_type=jnp.float32)
        return main, jnp.concatenate([turned_tail(main), corner], axis=0)

    put(times(0), approx)

    def step(_, carry):
        product, approx = times(0), times(BG)
        put(product, approx)
        return carry

    lax.fori_loop(0, ITERS - 2, step, 0, unroll=True)
    main, tail = times(BG)
    out[0], out[1] = split(jnp.concatenate([main, tail], axis=1))
    rows[...] = half_rows(left[c], out)


def g_side(pieces, running, left, token_total):
    return pl.pallas_call(
        functools.partial(g_side_kernel, token_total=token_total),
        out_shape=[jax.ShapeDtypeStruct((2, BG, BGP), jnp.bfloat16), HALF],
        in_specs=[VMEM] * 6,
        out_specs=[VMEM] * 2,
        scratch_shapes=[
            pltpu.VMEM((G_TILES, 8, 128), jnp.float32),
            pltpu.VMEM((2 * BG, 3 * BGP), jnp.bfloat16),
            pltpu.VMEM((3 * BGP, 256), jnp.bfloat16),
            pltpu.VMEM((3 * BGP, 128), jnp.bfloat16),
        ],
        compiler_params=pltpu.CompilerParams(vmem_limit_bytes=16 << 20),
        cost_estimate=pl.CostEstimate(flops=6_000_000_000, bytes_accessed=3_000_000, transcendentals=0),
    )(*pieces, running, left)


def apply_kernel(left, theirs, rows):
    rows[...] = half_rows(left[1 - lax.axis_index("c")], theirs)


def assemble_kernel(*refs):
    first, second, out = refs[:4], refs[4:8], refs[8]
    c, y = lax.axis_index("c"), lax.axis_index("y")
    for s in range(4):
        mine, theirs = first[s][...], second[s][...]
        halves = jnp.where(c == 0, mine, theirs), jnp.where(c == 0, theirs, mine)
        start = pl.multiple_of(lax.rem(y + 4 - s, 4) * BA, BA)
        for h in range(2):
            out[pl.ds(start + h * 128, 128), :] = jnp.concatenate(
                [half[:, h * BG:(h + 1) * BG] for half in halves], axis=1
            )


def per_device(activations, out_grads, a_running, g_running, grad_partial):
    token_total = float(activations.shape[0] * 256)
    y = lax.axis_index("y")

    near_x = pack(near_x_kernel, 8, [X_CHUNK] * 2, out_grads)
    near_x, activations = lax.optimization_barrier((near_x, activations))
    near_y = pack(near_y_kernel, 12, [Y_CHUNK] * 2, activations, grad_partial)
    near_y, out_grads = lax.optimization_barrier((near_y, out_grads))
    far_x, far_y, own_x, own_y, a_previous = pack(
        rest_kernel, 21, [X_CHUNK, Y_CHUNK, X_CHUNK, Y_CHUNK, PREVIOUS],
        out_grads, activations, grad_partial, a_running,
    )
    g_in = [send(near_x[0], "x", 1), send(near_x[1], "x", 3)]
    y_in = [send(near_y[0], "y", 1), send(near_y[1], "y", 3)]
    g_in, far_x = lax.optimization_barrier((g_in, far_x))
    g_in, y_in, far_y = lax.optimization_barrier((g_in, y_in, far_y))
    far_x, far_y = send(far_x, "x", 2), send(far_y, "y", 2)

    g_before = g_cov_first([own_x, *g_in])
    a_before = a_cov_first([own_y, *y_in])
    far_x, far_y = lax.optimization_barrier((far_x, far_y))
    a_own, a_other = a_cov(far_y, a_before)
    far_x, a_own, a_other = lax.optimization_barrier((far_x, a_own, a_other))
    g_own, g_other = g_cov(far_x, g_before)
    cut = local(
        cores_kernel, [tile_shape(4, 14)] * 4 + [tile_shape(2, 9)] * 4,
        g_own, swap_cores(g_other), a_own, swap_cores(a_other),
    )
    lines = lax.optimization_barrier(send_round("y", cut[:4]) + send_round("x", cut[4:]))
    keep, turn = local(lines_kernel, [tile_shape(37)] * 2, *lines)
    cut = local(pairs_kernel, [tile_shape(16)] * 4, keep, swap_pair(turn))
    g_piece, a_piece = local(pieces_kernel, [tile_shape(7), tile_shape(9)], *send_round("zh", cut))

    a_pieces = send_round("x", [a_piece] * 4)
    g_pair = local(join_kernel, tile_shape(14), g_piece, swap_pair(g_piece))
    g_pieces = send_round("y", [g_pair] * 4)
    left = a_side(a_pieces, a_previous, [own_y, *y_in, far_y], token_total)
    g_pieces, left = lax.optimization_barrier((g_pieces, left))
    inverse, first = g_side(g_pieces, g_running, left, token_total)
    second = local(apply_kernel, HALF, left, swap_cores(inverse))
    parts = send_round("y", [first] * 4) + send_round("y", [second] * 4)
    return local(assemble_kernel, jax.ShapeDtypeStruct((4 * BA, 2 * BG), jnp.bfloat16), *parts)


def solution(mesh):
    fine = Mesh(mesh.devices.reshape(4, 4, 2, 2, 4), ("zh", "x", "zl", "c", "y"))
    tokens = P(("zh", "x", "zl", "c", "y"), None)
    placed = (tokens, tokens, P(), P(("zh", "x"), None, None), P("y", ("zl", "c"), ("zh", "x")))
    return jax.shard_map(
        per_device,
        mesh=fine,
        in_specs=placed,
        out_specs=P(("zl", "c"), ("zh", "x")),
        check_vma=False,
    )
```

```python
import functools

import jax
import jax.numpy as jnp
from jax import lax
from jax.experimental import pallas as pl
from jax.experimental.pallas import tpu as pltpu
from jax.sharding import Mesh, PartitionSpec as P

BA = 256
BG = 320
BGP = 384
ITERS = 8
G_TILES = 56
A_TILES = 36

factor_decay = 0.9
damping = 0.1

VMEM = pl.BlockSpec(memory_space=pltpu.VMEM)


def swap_cores(value):
    return lax.ppermute(value, "c", [(0, 1), (1, 0)])


def send(value, axis, s):
    return lax.ppermute(value, axis, [(i, (i + s) % 4) for i in range(4)])


def swap_pair(value):
    return lax.ppermute(value, "zl", [(0, 1), (1, 0)])


def send_round(axis, chunks):
    return [chunks[0]] + [send(chunks[s], axis, s) for s in range(1, 4)]


def run_copies(pairs, sem):
    copies = [pltpu.make_async_copy(src, dst, sem.at[i]) for i, (src, dst) in enumerate(pairs)]
    for copy in copies:
        copy.start()
    for copy in copies:
        copy.wait()


def x_chunk(src, s, out):
    peer = lax.rem(lax.axis_index("x") + s, 4)
    for q in range(4):
        start = pl.multiple_of((q * 4 + peer) * 2 * BG, 128)
        yield src.at[:, pl.ds(start, 2 * BG)], out.at[q]


def y_chunk(samples, grads, s, out):
    peer = lax.rem(lax.axis_index("y") + s, 4)
    for q in range(4):
        start = pl.multiple_of((q * 4 + peer) * BA, 128)
        yield samples.at[:, pl.ds(start, BA)], out.at[:, pl.ds(q * BA, BA)]
    for h in range(2):
        start = pl.multiple_of(peer * BA + h * 128, 128)
        yield grads.at[0, pl.ds(start, 128), :], out.at[:, pl.ds(4 * BA + h * 2 * BG, 2 * BG)]


def near_kernel(src, samples, grads, x1, x3, y1, y3, sem):
    run_copies([
        *x_chunk(src, 1, x1), *x_chunk(src, 3, x3),
        *y_chunk(samples, grads, 1, y1), *y_chunk(samples, grads, 3, y3),
    ], sem)


def rest_kernel(src, samples, grads, running, far_x, far_y, own_x, own_y, previous, sem):
    zl, c, y = (lax.axis_index(name) for name in ("zl", "c", "y"))
    run_copies([
        *x_chunk(src, 2, far_x), *y_chunk(samples, grads, 2, far_y),
        *x_chunk(src, 0, own_x), *y_chunk(samples, grads, 0, own_y),
        (running.at[(zl * 2 + c) * 4 + y], previous),
    ], sem)


X_CHUNK = jax.ShapeDtypeStruct((4, 128, 2 * BG), jnp.bfloat16)
Y_CHUNK = jax.ShapeDtypeStruct((128, 4 * BA + 4 * BG), jnp.bfloat16)
PREVIOUS = jax.ShapeDtypeStruct((BA, BA), jnp.float32)


def pack(kernel, count, out_shape, *args):
    return pl.pallas_call(
        kernel,
        out_shape=out_shape,
        in_specs=[pl.BlockSpec(memory_space=pl.ANY)] * len(args),
        out_specs=[VMEM] * len(out_shape),
        scratch_shapes=[pltpu.SemaphoreType.DMA((count,))],
    )(*args)


def gram(v):
    return lax.dot_general(v, v, (((0,), (0,)), ((), ())), preferred_element_type=jnp.float32)


def grid_of(n):
    return (lax.broadcasted_iota(jnp.int32, (n, n), 0), lax.broadcasted_iota(jnp.int32, (n, n), 1))


def fold_block(cov, tiles, n):
    r, k = grid_of(128)
    corner = cov[128:256, 128:256]
    fold = jnp.where(r >= k, cov[0:128, 0:128], corner)
    diag = jnp.sum(jnp.where(r == k, corner, 0.0), axis=0, keepdims=True)
    tiles[n, 0:16] = fold.reshape(16, 8, 128)
    tiles[n, 16:32] = cov[128:256, 0:128].reshape(16, 8, 128)
    tiles[n, 32:40] = cov[256:BG, 0:128].reshape(8, 8, 128)
    tiles[n, 40:48] = cov[256:BG, 128:256].reshape(8, 8, 128)
    beside = jnp.concatenate([
        jnp.broadcast_to(diag[:, 0:64], (8, 64)),
        jnp.broadcast_to(diag[:, 64:128], (8, 64)),
        jnp.zeros((48, 64), jnp.float32),
    ], axis=0)
    tiles[n, 48:56] = jnp.concatenate([cov[256:BG, 256:BG], beside], axis=1).reshape(8, 8, 128)


def g_cov_kernel(i0, own_before, other_before, own, other, rows, tiles):
    c = lax.axis_index("c")
    for q in range(4):
        rows[q] = i0[q]
        fold_block(gram(rows[q, :, 0:BGP]), tiles.at[q], 0)
        fold_block(gram(rows[q, :, 2 * BG - BGP:2 * BG])[BGP - BG:, BGP - BG:], tiles.at[q], 1)
        own[q] = tiles[q, c] + own_before[q]
        other[q] = tiles[q, 1 - c] + other_before[q]


def g_cov_first_kernel(i0, i1, i2, own, other, rows, tiles):
    c = lax.axis_index("c")
    for q in range(4):
        for s, ref in enumerate((i0, i1, i2)):
            rows[q, s * 128:(s + 1) * 128, :] = ref[q]
        fold_block(gram(rows[q, :, 0:BGP]), tiles.at[q], 0)
        fold_block(gram(rows[q, :, 2 * BG - BGP:2 * BG])[BGP - BG:, BGP - BG:], tiles.at[q], 1)
        own[q] = tiles[q, c]
        other[q] = tiles[q, 1 - c]


def a_cov_blocks(chunks, rows, tiles):
    r, k = grid_of(128)
    for zl in range(2):
        for core in range(2):
            q = zl * 2 + core
            for s, ref in enumerate(chunks):
                rows[s * 128:(s + 1) * 128, :] = ref[:, q * BA:(q + 1) * BA]
            cov = gram(rows[...])
            corner = cov[128:, 128:]
            fold = jnp.where(r >= k, cov[:128, :128], corner)
            diag = jnp.sum(jnp.where(r == k, corner, 0.0), axis=0, keepdims=True)
            tiles[core, 0:16] = cov[128:, :128].reshape(16, 8, 128)
            tiles[core, 16:32] = fold.reshape(16, 8, 128)
            tiles[core, 32] = jnp.broadcast_to(diag, (8, 128))
            tiles[core, 33:] = jnp.zeros((A_TILES - 33, 8, 128), jnp.float32)
        yield zl


def a_cov_first_kernel(i0, i1, i2, own, other, rows, tiles):
    c = lax.axis_index("c")
    for zl in a_cov_blocks((i0, i1, i2), rows, tiles):
        own[zl] = tiles[c]
        other[zl] = tiles[1 - c]


def a_cov_kernel(i0, own_before, other_before, own, other, rows, tiles):
    c = lax.axis_index("c")
    for zl in a_cov_blocks((i0,), rows, tiles):
        own[zl] = tiles[c] + own_before[zl]
        other[zl] = tiles[1 - c] + other_before[zl]


def cov(kernel, out_dims, rows, tiles, *args):
    return pl.pallas_call(
        kernel,
        out_shape=[jax.ShapeDtypeStruct((*out_dims, 8, 128), jnp.float32)] * 2,
        in_specs=[VMEM] * len(args),
        out_specs=[VMEM] * 2,
        scratch_shapes=[pltpu.VMEM(rows, jnp.bfloat16), pltpu.VMEM((*tiles, 8, 128), jnp.float32)],
        compiler_params=pltpu.CompilerParams(vmem_limit_bytes=16 << 20),
        cost_estimate=pl.CostEstimate(flops=1_500_000_000, bytes_accessed=4_000_000, transcendentals=0),
    )(*args)


def g_cov_first(chunks):
    return cov(g_cov_first_kernel, (4, 56), (4, 384, 2 * BG), (4, 2, G_TILES), *chunks)


def g_cov(chunk, before):
    return cov(g_cov_kernel, (4, 56), (4, 128, 2 * BG), (4, 2, G_TILES), chunk, *before)


def a_cov_first(chunks):
    return cov(a_cov_first_kernel, (2, A_TILES), (384, BA), (2, A_TILES), *chunks)


def a_cov(chunk, before):
    return cov(a_cov_kernel, (2, A_TILES), (128, BA), (2, A_TILES), chunk, *before)


def tile_shape(*dims):
    return jax.ShapeDtypeStruct((*dims, 8, 128), jnp.float32)


def local(kernel, out_shape, *args):
    return pl.pallas_call(
        kernel,
        out_shape=out_shape,
        in_specs=[VMEM] * len(args),
        out_specs=jax.tree.map(lambda _: VMEM, out_shape),
        compiler_params=pltpu.CompilerParams(vmem_limit_bytes=16 << 20),
    )(*args)


def cores_kernel(g_own, g_got, a_own, a_got, *outs):
    x, y = lax.axis_index("x"), lax.axis_index("y")
    for s in range(4):
        place = pl.ds(lax.rem(y + s, 4) * 14, 14)
        outs[s][...] = g_own[:, place] + g_got[:, place]
        place = pl.ds(lax.rem(x + s, 4) * 9, 9)
        outs[4 + s][...] = a_own[:, place] + a_got[:, place]


def lines_kernel(g0, g1, g2, g3, a0, a1, a2, a3, keep, turn):
    zl = lax.axis_index("zl")
    for out, side in ((keep, zl), (turn, 1 - zl)):
        for q in range(4):
            place = pl.ds(side * 7, 7)
            out[q * 7:q * 7 + 7] = (g0[q, place] + g1[q, place]) + (g2[q, place] + g3[q, place])
        out[28:] = (a0[side] + a1[side]) + (a2[side] + a3[side])


def pairs_kernel(keep, got, *outs):
    zh = lax.axis_index("zh")
    a_sum = keep[28:] + got[28:]
    for s in range(4):
        place = pl.ds(lax.rem(zh + s, 4) * 7, 7)
        outs[s][0:7] = keep[place] + got[place]
        outs[s][7:] = a_sum


def pieces_kernel(p0, p1, p2, p3, g_piece, a_piece):
    g_piece[...] = (p0[0:7] + p1[0:7]) + (p2[0:7] + p3[0:7])
    a_piece[...] = (p0[7:] + p1[7:]) + (p2[7:] + p3[7:])


def join_kernel(own, got, out):
    zl = lax.axis_index("zl")
    out[pl.ds(zl * 7, 7)] = own[...]
    out[pl.ds((1 - zl) * 7, 7)] = got[...]


def split(value):
    high = value.astype(jnp.bfloat16)
    return high, (value - high.astype(jnp.float32)).astype(jnp.bfloat16)


def dot3(left, right):
    dot = functools.partial(jnp.dot, preferred_element_type=jnp.float32)
    return dot(left[0], right[0]) + (dot(left[0], right[1]) + dot(left[1], right[0]))


def three(value):
    high, low = split(value)
    return high, high, low


def newton_even(matrix, identity, lhs, rhs):
    n = identity.shape[0]

    def put(approx, product):
        high, low = split(2.0 * identity - product)
        rhs[0:n], rhs[n:2 * n], rhs[2 * n:3 * n] = high, low, high
        for i, part in enumerate(three(product)):
            lhs[0:n, i * n:(i + 1) * n] = part
        for i, part in enumerate(three(approx)):
            lhs[n:2 * n, i * n:(i + 1) * n] = part

    trace = jnp.sum(matrix * identity)
    scaled = matrix / trace
    approx = (2.0 * identity - scaled) / trace
    put(approx, scaled)
    put(approx, jnp.dot(lhs[0:n], rhs[...], preferred_element_type=jnp.float32))

    def step(_, carry):
        both = jnp.dot(lhs[...], rhs[...], preferred_element_type=jnp.float32)
        put(both[n:], both[:n])
        return carry

    lax.fori_loop(0, ITERS - 2, step, 0)
    return jnp.dot(lhs[n:2 * n], rhs[...], preferred_element_type=jnp.float32)


def a_side_kernel(p0, p1, p2, p3, running, g0, g1, g2, g3, left, tiles, lhs, rhs, *, token_total):
    x = lax.axis_index("x")
    for s, got in enumerate((p0, p1, p2, p3)):
        tiles[pl.ds(lax.rem(x + 4 - s, 4) * 9, 9)] = got[...]
    r, k = grid_of(128)
    low = tiles[0:16].reshape(128, 128)
    fold = tiles[16:32].reshape(128, 128)
    diag = tiles[32][0:1]
    turned = fold.T
    top = jnp.where(r >= k, fold, turned)
    corner = jnp.where(r == k, jnp.broadcast_to(diag, (128, 128)), jnp.where(r < k, fold, turned))
    cov = jnp.concatenate([
        jnp.concatenate([top, low.T], axis=1), jnp.concatenate([low, corner], axis=1)
    ], axis=0)
    r, k = grid_of(BA)
    identity = jnp.where(r == k, 1.0, 0.0)
    mixed = factor_decay * running[...] + (1.0 - factor_decay) * cov / token_total
    inverse = newton_even(mixed + damping * identity, identity, lhs, rhs)
    summed = []
    for h in range(2):
        begin = 4 * BA + h * 2 * BG
        g = [ref[:, begin:begin + 2 * BG].astype(jnp.float32) for ref in (g0, g1, g2, g3)]
        summed.append((g[0] + g[1]) + (g[2] + g[3]))
    summed = jnp.concatenate(summed, axis=0)
    done = dot3(split(inverse), split(summed))
    for n in range(2):
        left[n] = done[:, n * BG:(n + 1) * BG]


def a_side(pieces, running, grads, token_total):
    return pl.pallas_call(
        functools.partial(a_side_kernel, token_total=token_total),
        out_shape=jax.ShapeDtypeStruct((2, BA, BG), jnp.float32),
        in_specs=[VMEM] * 9,
        out_specs=VMEM,
        scratch_shapes=[
            pltpu.VMEM((A_TILES, 8, 128), jnp.float32),
            pltpu.VMEM((2 * BA, 3 * BA), jnp.bfloat16), pltpu.VMEM((3 * BA, BA), jnp.bfloat16)
        ],
        compiler_params=pltpu.CompilerParams(vmem_limit_bytes=16 << 20),
        cost_estimate=pl.CostEstimate(flops=2_500_000_000, bytes_accessed=2_000_000, transcendentals=0),
    )(*pieces, running, *grads)


def turned_tail(main):
    tail = main[256:BG]
    return jnp.concatenate([tail, jnp.zeros_like(tail)], axis=0).T


HALF = jax.ShapeDtypeStruct((128, 2 * BG), jnp.bfloat16)


def unfold_block(tiles):
    r, k = grid_of(128)
    fold = tiles[0:16].reshape(128, 128)
    low = tiles[16:32].reshape(128, 128)
    last = tiles[48:56].reshape(64, 128)
    diag = jnp.concatenate([last[0:1, 64:128], last[8:9, 64:128]], axis=1)
    turned = fold.T
    first = jnp.where(r >= k, fold, turned)
    second = jnp.where(r == k, jnp.broadcast_to(diag, (128, 128)), jnp.where(r < k, fold, turned))
    bottom = [tiles[32:40].reshape(64, 128), tiles[40:48].reshape(64, 128)]
    main = jnp.concatenate([
        jnp.concatenate([first, low.T], axis=1),
        jnp.concatenate([low, second], axis=1),
        jnp.concatenate(bottom, axis=1),
    ], axis=0)
    empty = jnp.zeros((64, 128), jnp.float32)
    r, k = lax.broadcasted_iota(jnp.int32, (64, 128), 0), lax.broadcasted_iota(jnp.int32, (64, 128), 1)
    tail = jnp.concatenate([jnp.concatenate([part, empty], axis=0).T for part in bottom]
                           + [jnp.where(k < 64, last, 0.0)], axis=0)
    return main, tail


def g_put(lhs, rhs_main, rhs_tail, ident, product, approx):
    for rhs, same, value in ((rhs_main, ident[0], product[0]), (rhs_tail, ident[1], product[1])):
        high, low = split(2.0 * same - value)
        rhs[0:BG] = high
        rhs[BGP:BGP + BG] = low
        rhs[2 * BGP:2 * BGP + BG] = high
    for row, (main, tail) in ((0, product), (BG, approx)):
        for i, (part, edge) in enumerate(zip(three(main), three(tail))):
            lhs[row:row + BG, i * BGP:i * BGP + 256] = part
            lhs[row:row + BG, i * BGP + 256:(i + 1) * BGP] = edge


def half_rows(left, inverse):
    done = dot3(split(left), (inverse[0], inverse[1]))[:, 0:BG].astype(jnp.bfloat16)
    return jnp.concatenate([done[0:128], done[128:BA]], axis=1)


def g_side_kernel(p0, p1, p2, p3, running, left, out, rows, tiles, lhs, rhs_main, rhs_tail, *, token_total):
    c, y = lax.axis_index("c"), lax.axis_index("y")
    for s, got in enumerate((p0, p1, p2, p3)):
        tiles[pl.ds(lax.rem(y + 4 - s, 4) * 14, 14)] = got[...]
    new_sum = unfold_block(tiles)
    previous = running[c, :, 0:256], jnp.concatenate(
        [running[c, :, 256:BG], jnp.zeros((BG, 64), jnp.float32)], axis=1
    )
    r, k = lax.broadcasted_iota(jnp.int32, (BG, 256), 0), lax.broadcasted_iota(jnp.int32, (BG, 256), 1)
    ident = [jnp.where(r == k, 1.0, 0.0)]
    r, k = lax.broadcasted_iota(jnp.int32, (BG, 128), 0), lax.broadcasted_iota(jnp.int32, (BG, 128), 1)
    ident.append(jnp.where(r == k + 256, 1.0, 0.0))
    matrix = [
        (factor_decay * before + (1.0 - factor_decay) * cov / token_total) + damping * same
        for before, cov, same in zip(previous, new_sum, ident)
    ]
    trace = sum(jnp.sum(part * same) for part, same in zip(matrix, ident))
    rhs_main[...] = jnp.zeros(rhs_main.shape, jnp.bfloat16)
    rhs_tail[...] = jnp.zeros(rhs_tail.shape, jnp.bfloat16)
    put = functools.partial(g_put, lhs, rhs_main, rhs_tail, ident)
    scaled = [part / trace for part in matrix]
    approx = [(2.0 * same - part) / trace for same, part in zip(ident, scaled)]
    put(scaled, approx)

    def times(row):
        main = jnp.dot(lhs[row:row + BG], rhs_main[...], preferred_element_type=jnp.float32)
        corner = jnp.dot(lhs[row + 256:row + BG], rhs_tail[...], preferred_element_type=jnp.float32)
        return main, jnp.concatenate([turned_tail(main), corner], axis=0)

    put(times(0), approx)

    def step(_, carry):
        product, approx = times(0), times(BG)
        put(product, approx)
        return carry

    lax.fori_loop(0, ITERS - 2, step, 0, unroll=True)
    main, tail = times(BG)
    out[0], out[1] = split(jnp.concatenate([main, tail], axis=1))
    rows[...] = half_rows(left[c], out)


def g_side(pieces, running, left, token_total):
    return pl.pallas_call(
        functools.partial(g_side_kernel, token_total=token_total),
        out_shape=[jax.ShapeDtypeStruct((2, BG, BGP), jnp.bfloat16), HALF],
        in_specs=[VMEM] * 6,
        out_specs=[VMEM] * 2,
        scratch_shapes=[
            pltpu.VMEM((G_TILES, 8, 128), jnp.float32),
            pltpu.VMEM((2 * BG, 3 * BGP), jnp.bfloat16),
            pltpu.VMEM((3 * BGP, 256), jnp.bfloat16),
            pltpu.VMEM((3 * BGP, 128), jnp.bfloat16),
        ],
        compiler_params=pltpu.CompilerParams(vmem_limit_bytes=16 << 20),
        cost_estimate=pl.CostEstimate(flops=6_000_000_000, bytes_accessed=3_000_000, transcendentals=0),
    )(*pieces, running, left)


def apply_kernel(left, theirs, rows):
    rows[...] = half_rows(left[1 - lax.axis_index("c")], theirs)


def assemble_kernel(*refs):
    first, second, out = refs[:4], refs[4:8], refs[8]
    c, y = lax.axis_index("c"), lax.axis_index("y")
    for s in range(4):
        mine, theirs = first[s][...], second[s][...]
        halves = jnp.where(c == 0, mine, theirs), jnp.where(c == 0, theirs, mine)
        start = pl.multiple_of(lax.rem(y + 4 - s, 4) * BA, BA)
        for h in range(2):
            out[pl.ds(start + h * 128, 128), :] = jnp.concatenate(
                [half[:, h * BG:(h + 1) * BG] for half in halves], axis=1
            )


def per_device(activations, out_grads, a_running, g_running, grad_partial):
    token_total = float(activations.shape[0] * 256)
    y = lax.axis_index("y")

    near = pack(near_kernel, 20, [X_CHUNK] * 2 + [Y_CHUNK] * 2, out_grads, activations, grad_partial)
    near, out_grads = lax.optimization_barrier((near, out_grads))
    near_x, near_y = near[:2], near[2:]
    far_x, far_y, own_x, own_y, a_previous = pack(
        rest_kernel, 21, [X_CHUNK, Y_CHUNK, X_CHUNK, Y_CHUNK, PREVIOUS],
        out_grads, activations, grad_partial, a_running,
    )
    g_in = [send(near_x[0], "x", 1), send(near_x[1], "x", 3)]
    y_in = [send(near_y[0], "y", 1), send(near_y[1], "y", 3)]
    g_in, far_x = lax.optimization_barrier((g_in, far_x))
    g_in, y_in, far_y = lax.optimization_barrier((g_in, y_in, far_y))
    far_x, far_y = send(far_x, "x", 2), send(far_y, "y", 2)

    g_before = g_cov_first([own_x, *g_in])
    a_before = a_cov_first([own_y, *y_in])
    far_x, far_y = lax.optimization_barrier((far_x, far_y))
    a_own, a_other = a_cov(far_y, a_before)
    far_x, a_own, a_other = lax.optimization_barrier((far_x, a_own, a_other))
    g_own, g_other = g_cov(far_x, g_before)
    cut = local(
        cores_kernel, [tile_shape(4, 14)] * 4 + [tile_shape(2, 9)] * 4,
        g_own, swap_cores(g_other), a_own, swap_cores(a_other),
    )
    lines = lax.optimization_barrier(send_round("y", cut[:4]) + send_round("x", cut[4:]))
    keep, turn = local(lines_kernel, [tile_shape(37)] * 2, *lines)
    cut = local(pairs_kernel, [tile_shape(16)] * 4, keep, swap_pair(turn))
    g_piece, a_piece = local(pieces_kernel, [tile_shape(7), tile_shape(9)], *send_round("zh", cut))

    a_pieces = send_round("x", [a_piece] * 4)
    g_pair = local(join_kernel, tile_shape(14), g_piece, swap_pair(g_piece))
    g_pieces = send_round("y", [g_pair] * 4)
    left = a_side(a_pieces, a_previous, [own_y, *y_in, far_y], token_total)
    g_pieces, left = lax.optimization_barrier((g_pieces, left))
    inverse, first = g_side(g_pieces, g_running, left, token_total)
    second = local(apply_kernel, HALF, left, swap_cores(inverse))
    parts = send_round("y", [first] * 4) + send_round("y", [second] * 4)
    return local(assemble_kernel, jax.ShapeDtypeStruct((4 * BA, 2 * BG), jnp.bfloat16), *parts)


def solution(mesh):
    fine = Mesh(mesh.devices.reshape(4, 4, 2, 2, 4), ("zh", "x", "zl", "c", "y"))
    tokens = P(("zh", "x", "zl", "c", "y"), None)
    placed = (tokens, tokens, P(), P(("zh", "x"), None, None), P("y", ("zl", "c"), ("zh", "x")))
    return jax.shard_map(
        per_device,
        mesh=fine,
        in_specs=placed,
        out_specs=P(("zl", "c"), ("zh", "x")),
        check_vma=False,
    )
```
